32 devices in a mesh: groups: 2 (over y), seq: 16 (over z, x, core).
Axes of the slice: x: 2, y: 2, z: 4, core: 2. Of those that a mesh axis runs over, the one named last changes fastest.
Arguments:
- residual: bfloat16 [8192, 1024], P(('groups', 'seq')), parts along dimension 0, may hold values from -6 to 6
- layer_queries: bfloat16 [8192, 512], P(('groups', 'seq')), parts along dimension 0, may hold values from -200 to 200
- layer_keyvals: bfloat16 [8192, 256], P(('groups', 'seq')), parts along dimension 0, may hold values from -8 to 8
- head_window_extent: int32 [8], replicated, may hold values from 32 to 256, as said below
- block_mask: int32 [16, 4], P('seq'), may hold values 0 or 1
- first_out: bfloat16 [512, 1024], replicated, may hold values from -1 to 1
- second_query: bfloat16 [1024, 512], replicated, may hold values from -12 to 12
- second_keyval: bfloat16 [1024, 256], replicated, may hold values from -1 to 1
- second_out: bfloat16 [512, 1024], replicated, may hold values from -1 to 1
Outputs:
- layer_output: bfloat16 [8192, 1024], P(('groups', 'seq')), parts along dimension 0
The draws below stay inside these ranges and needn't reach their ends.
There are 2 independent parts, one for each index of `groups`. The reference program is written for one: setup_inputs(seed, part) draws one part's arguments, and reference() takes and returns one part's arrays. A program takes and returns all parts, laid end to end along the dimension named above; an argument that names none is the same for every part. Nothing has to cross between parts.
Inputs may be any that keep to these rules, and one draw needn't show every extreme that they name: `head_window_extent`: per head; some head has exactly 256 and some exactly 32.
All inputs are finite; a program needn't handle non-finite values. No bound on the sum of `block_mask` on one device may be relied on, other than what follows from the above.
Results may differ from the reference program's by a relative error of at most 0.0065.
Values may be sent and summed in bfloat16 or wider, within the bound.
No kernel may reach another device: no remote copies, remote signals or barrier semaphores. Data moves between devices by JAX's collectives and lax.ppermute only.
A program may use at most 64 MiB of HBM per device.

```python
import jax
import jax.numpy as jnp
from jax import lax

MODEL_WIDTH = 1024
QUERY_HEADS = 8
KEY_VALUE_HEADS = 2
HEAD_SIZE = 64
TOK_DEV = 256
WIN = 256
LEVELS = 4
NB = 16
SEQUENCE_TOKENS = 4096


def draw_pair(key):
    key_q, random_key_keys = jax.random.split(jax.random.fold_in(key, 11), 2)
    query_matrix = jnp.clip(jax.random.normal(key_q, (SEQUENCE_TOKENS, QUERY_HEADS * HEAD_SIZE), jnp.float32), -6.0, 6.0)
    key_value_pairs = jnp.clip(jax.random.normal(random_key_keys, (SEQUENCE_TOKENS, 2 * KEY_VALUE_HEADS * HEAD_SIZE), jnp.float32), -6.0, 6.0)
    return (query_matrix, key_value_pairs)


def draw_layer_queries(key, part):
    return draw_pair(key)[0].astype(jnp.bfloat16)


def draw_layer_keyvals(key, part):
    return draw_pair(key)[1].astype(jnp.bfloat16)


def draw_head_window_extent(key, part):
    key_p, key_r = jax.random.split(jax.random.fold_in(key, 31))
    order = jax.random.permutation(key_p, QUERY_HEADS)
    window_extent = jax.random.randint(key_r, (QUERY_HEADS,), WIN // 8, WIN + 1)
    window_extent = window_extent.at[order[0]].set(WIN).at[order[1]].set(WIN // 8)
    return window_extent.astype(jnp.int32)


def draw_projections(key):
    key_q, random_key_keys = jax.random.split(jax.random.fold_in(key, 23), 2)
    w_query = jnp.clip(jax.random.normal(key_q, (MODEL_WIDTH, QUERY_HEADS * HEAD_SIZE), jnp.float32), -6.0, 6.0) * MODEL_WIDTH ** (-0.5)
    key_value_weight = jnp.clip(jax.random.normal(random_key_keys, (MODEL_WIDTH, 2 * KEY_VALUE_HEADS * HEAD_SIZE), jnp.float32), -6.0, 6.0) * MODEL_WIDTH ** (-0.5)
    return (w_query, key_value_weight)


def draw_second_query(key, part):
    return draw_projections(key)[0].astype(jnp.bfloat16)


def draw_second_keyval(key, part):
    return draw_projections(key)[1].astype(jnp.bfloat16)


def set_ends(entries, stream_key, least, largest):
    longest = entries.shape.index(max(entries.shape))
    spots = []
    for shift in (0, 1):
        where = [jax.random.randint(jax.random.fold_in(stream_key, axis), (), 0, length) for axis, length in enumerate(entries.shape)]
        where[longest] = (where[longest] + shift) % entries.shape[longest]
        spots.append(tuple(where))
    return entries.at[spots[0]].set(least).at[spots[1]].set(largest)


def level_of(rng, extent, pieces, least, largest):
    def one(axis_at, parts):
        heights = jax.random.uniform(jax.random.fold_in(jax.random.fold_in(rng, 6), axis_at), (parts,), jnp.float32, least / len(pieces), largest / len(pieces))
        return jnp.repeat(jnp.exp(heights), extent[axis_at] // parts).reshape((-1,) + (1,) * (len(extent) - axis_at - 1))

    level = one(*pieces[0])
    for cut in pieces[1:]:
        level = level * one(*cut)
    return level


def centred(rng, dims, scale, most, cuts=(), kind=jnp.bfloat16):
    entries = scale * jax.random.normal(rng, dims, jnp.float32)
    if cuts:
        entries = entries * level_of(rng, dims, cuts, -0.22, 0.18)
    return jnp.clip(entries, -most, most).astype(kind)


def setup_inputs(seed: int = 0, part: int = 0) -> dict:
    keys = jax.random.split(jax.random.key(seed), 10)
    part_splits = jax.random.split(jax.random.fold_in(keys[9], part), 10)
    residual = centred(part_splits[0], (SEQUENCE_TOKENS, MODEL_WIDTH), 1.0, 6.0, ((0, 16),))
    layer_queries = draw_layer_queries(jax.random.fold_in(jax.random.fold_in(keys[9], part), 71), part)
    layer_keyvals = draw_layer_keyvals(jax.random.fold_in(jax.random.fold_in(keys[9], part), 71), part)
    head_window_extent = draw_head_window_extent(jax.random.fold_in(keys[9], 71), part)
    block_mask = set_ends((jax.random.randint(keys[4], (NB, LEVELS), 0, 4) < 3).astype(jnp.int32), jax.random.fold_in(keys[4], 1), 0, 1)
    first_out = centred(keys[5], (QUERY_HEADS * HEAD_SIZE, MODEL_WIDTH), (QUERY_HEADS * HEAD_SIZE // 16) ** -0.5, 1.0)
    second_query = draw_second_query(jax.random.fold_in(keys[9], 71), part)
    second_keyval = draw_second_keyval(jax.random.fold_in(keys[9], 71), part)
    second_out = centred(keys[8], (QUERY_HEADS * HEAD_SIZE, MODEL_WIDTH), (QUERY_HEADS * HEAD_SIZE // 16) ** -0.5, 1.0)
    return dict(residual=residual, layer_queries=layer_queries, layer_keyvals=layer_keyvals, head_window_extent=head_window_extent, block_mask=block_mask, first_out=first_out, second_query=second_query, second_keyval=second_keyval, second_out=second_out)


def norm_rows(hidden):
    values = hidden.astype(jnp.float32)
    scale = lax.rsqrt(lax.optimization_barrier(jnp.mean(values * values, axis=-1, keepdims=True)) + 1e-05)
    return (values * scale).astype(jnp.bfloat16)

def attend_rows(query_matrix, key_row_matrix, value_row_matrix, allowed):
    count_of_rows = query_matrix.shape[0]
    count_of_keys = key_row_matrix.shape[0]
    heads_per_group = QUERY_HEADS // KEY_VALUE_HEADS
    query_head_rows = query_matrix.reshape(count_of_rows, KEY_VALUE_HEADS, heads_per_group, HEAD_SIZE).astype(jnp.float32)
    key_head_rows = key_row_matrix.reshape(count_of_keys, KEY_VALUE_HEADS, HEAD_SIZE).astype(jnp.float32)
    value_head_rows = value_row_matrix.reshape(count_of_keys, KEY_VALUE_HEADS, HEAD_SIZE).astype(jnp.float32)
    scores = jnp.einsum('rkgd,jkd->kgrj', query_head_rows, key_head_rows) * HEAD_SIZE ** (-0.5)
    scores = jnp.where(allowed, scores, -1e+30)
    row_max = lax.optimization_barrier(jnp.max(scores, axis=-1, keepdims=True))
    weights = jnp.where(allowed, jnp.exp(scores - row_max), 0.0)
    shares = (weights / lax.optimization_barrier(jnp.sum(weights, axis=-1, keepdims=True))).astype(jnp.bfloat16)
    mixture = jnp.einsum('kgrj,jkd->rkgd', shares.astype(jnp.float32), value_head_rows)
    return mixture.reshape(count_of_rows, QUERY_HEADS * HEAD_SIZE).astype(jnp.bfloat16)

def reference(residual, layer_queries, layer_keyvals, head_window_extent, block_mask, first_out, second_query, second_keyval, second_out):
    key_value_width = KEY_VALUE_HEADS * HEAD_SIZE
    heads_per_group = QUERY_HEADS // KEY_VALUE_HEADS
    padded = jnp.pad(layer_keyvals, ((WIN, WIN), (0, 0)))
    window_extent = head_window_extent.reshape(KEY_VALUE_HEADS, heads_per_group, 1, 1)

    def window_block(block):
        first_row = block * TOK_DEV
        query_part = lax.dynamic_slice_in_dim(layer_queries, first_row, TOK_DEV, 0)
        key_portion = lax.dynamic_slice_in_dim(padded, first_row, TOK_DEV + 2 * WIN, 0)
        query_pos = first_row + jnp.arange(TOK_DEV, dtype=jnp.int32)
        key_pos = first_row - WIN + jnp.arange(TOK_DEV + 2 * WIN, dtype=jnp.int32)
        inside = (key_pos >= 0) & (key_pos < SEQUENCE_TOKENS)
        distance = jnp.abs(query_pos[:, None] - key_pos[None, :])
        allowed = (distance[None, None] <= window_extent) & inside[None, None, None, :]
        return attend_rows(query_part, key_portion[:, :key_value_width], key_portion[:, key_value_width:], allowed)
    attended = lax.map(window_block, jnp.arange(NB, dtype=jnp.int32)).reshape(SEQUENCE_TOKENS, QUERY_HEADS * HEAD_SIZE)
    hidden = (jnp.dot(attended, first_out, preferred_element_type=jnp.float32) + residual.astype(jnp.float32)).astype(jnp.bfloat16)
    normed = norm_rows(hidden)
    queries_two = jnp.dot(normed, second_query, preferred_element_type=jnp.float32).astype(jnp.bfloat16)
    keyvals_two = jnp.dot(normed, second_keyval, preferred_element_type=jnp.float32).astype(jnp.bfloat16)
    kv_blocks = keyvals_two.reshape(NB, TOK_DEV, 2 * key_value_width)
    level_bits = jnp.left_shift(jnp.ones((LEVELS,), jnp.int32), jnp.arange(LEVELS, dtype=jnp.int32))

    def butterfly_block(block):
        partners = jnp.bitwise_xor(block, level_bits)
        own_rows = kv_blocks[block]
        other_rows = kv_blocks[partners].reshape(LEVELS * TOK_DEV, 2 * key_value_width)
        key_portion = jnp.concatenate([own_rows, other_rows], axis=0)
        flags = jnp.concatenate([jnp.ones((1,), jnp.bool_), block_mask[block] == 1])
        allowed = jnp.repeat(flags, TOK_DEV)[None, None, None, :]
        query_part = lax.dynamic_slice_in_dim(queries_two, block * TOK_DEV, TOK_DEV, 0)
        return attend_rows(query_part, key_portion[:, :key_value_width], key_portion[:, key_value_width:], allowed)
    second = lax.map(butterfly_block, jnp.arange(NB, dtype=jnp.int32)).reshape(SEQUENCE_TOKENS, QUERY_HEADS * HEAD_SIZE)
    output = jnp.dot(second, second_out, preferred_element_type=jnp.float32) + hidden.astype(jnp.float32)
    return output.astype(jnp.bfloat16)
```

```python
import functools
import math

import jax
import jax.numpy as jnp
from jax import lax
from jax.experimental import pallas as pl
from jax.experimental.pallas import tpu as pltpu
from jax.sharding import PartitionSpec as P

HEAD_SIZE = 64
WIN = 256
LANES = 128
LOW = -1e30
SCALE = HEAD_SIZE**-0.5 * math.log2(math.e)


def dot(a, b):
    return jnp.dot(a, b, preferred_element_type=jnp.float32)


def dot_t(a, b):
    return lax.dot_general(a, b, (((1,), (1,)), ((), ())), preferred_element_type=jnp.float32)


def spread_keyvals(keyvals, keys_ref, values_ref, first):
    rows = keyvals.shape[0]
    kv_heads = keyvals.shape[1] // (2 * HEAD_SIZE)
    low = lax.broadcasted_iota(jnp.int32, (rows, LANES), 1) < HEAD_SIZE
    zero = jnp.zeros((rows, LANES), jnp.bfloat16)
    one = jnp.ones((rows, LANES), jnp.bfloat16)
    spot = pl.ds(first, rows)
    per_tile = LANES // HEAD_SIZE
    for g in range(kv_heads):
        tile, at = divmod(g, per_tile)
        k = keyvals[:, tile * LANES : (tile + 1) * LANES]
        v_first = kv_heads * HEAD_SIZE + tile * LANES
        v = keyvals[:, v_first : v_first + LANES]
        k_other = jnp.concatenate([k[:, HEAD_SIZE:], k[:, :HEAD_SIZE]], axis=1)
        v_other = jnp.concatenate([v[:, HEAD_SIZE:], v[:, :HEAD_SIZE]], axis=1)
        for s in range(2):
            here = low if s == 0 else jnp.logical_not(low)
            keys_ref[g, s, spot, :] = jnp.where(here, k if at == s else k_other, zero)
            values_ref[g, s, spot, :LANES] = jnp.where(here, v if at == s else v_other, zero)
            values_ref[g, s, spot, LANES:] = jnp.where(here, one, zero)


def window_kernel(
    extent_ref,
    q_ref,
    left_ref,
    own_ref,
    right_ref,
    residual_hbm,
    out_w_hbm,
    kv_w_hbm,
    hidden_ref,
    normed_ref,
    kv_ref,
    keys_ref,
    values_ref,
    attended_ref,
    residual_ref,
    out_w_ref,
    kv_w_ref,
    sems,
):
    copies = [
        pltpu.make_async_copy(src, dst, sems.at[n])
        for n, (src, dst) in enumerate(
            ((residual_hbm, residual_ref), (out_w_hbm, out_w_ref), (kv_w_hbm, kv_w_ref))
        )
    ]
    for copy in copies:
        copy.start()
    rows = q_ref.shape[0]
    step = LANES
    me = lax.axis_index("seq")
    last = lax.axis_size("seq") - 1
    spread_keyvals(left_ref[...], keys_ref, values_ref, 0)
    spread_keyvals(own_ref[...], keys_ref, values_ref, WIN)
    spread_keyvals(right_ref[...], keys_ref, values_ref, WIN + rows)
    span = step + 2 * WIN
    kv_heads = keys_ref.shape[0]
    pairs = q_ref.shape[1] // LANES
    row = lax.broadcasted_iota(jnp.int32, (step, step), 0)
    col = lax.broadcasted_iota(jnp.int32, (step, step), 1)
    gap = row - col
    for pair in range(pairs):
        g = pair * kv_heads // pairs
        for part in range(rows // step):
            first = part * step
            q = q_ref[pl.ds(first, step), pair * LANES : (pair + 1) * LANES]
            total = None
            for s in range(2):
                extent = extent_ref[2 * pair + s]
                scores = dot_t(q, keys_ref[g, s, pl.ds(first, span), :])
                tiles = []
                for t in range(span // step):
                    begin = first + t * step
                    reach = extent
                    if begin < WIN:
                        reach = jnp.where(me > 0, extent, -1)
                    elif begin >= WIN + rows:
                        reach = jnp.where(me < last, extent, -1)
                    offset = WIN - t * step
                    if offset > 0:
                        seen = gap <= reach - offset
                    elif offset < 0:
                        seen = gap >= -offset - reach
                    else:
                        seen = jnp.abs(gap) <= reach
                    tiles.append(jnp.where(seen, scores[:, t * step : (t + 1) * step], LOW))
                top = functools.reduce(jnp.maximum, tiles)
                top = jnp.max(top, axis=1, keepdims=True)
                weights = jnp.concatenate(
                    [jnp.exp2((tile - top) * SCALE).astype(jnp.bfloat16) for tile in tiles], axis=1
                )
                mix = dot(weights, values_ref[g, s, pl.ds(first, span), :])
                total = mix if total is None else total + mix
            attended_ref[pl.ds(first, step), pair * LANES : (pair + 1) * LANES] = (
                total[:, :LANES] / total[:, LANES:]
            ).astype(jnp.bfloat16)
    for copy in copies:
        copy.wait()
    hidden = (
        dot(attended_ref[...], out_w_ref[...]) + residual_ref[...].astype(jnp.float32)
    ).astype(jnp.bfloat16)
    hidden_ref[...] = hidden
    values = hidden.astype(jnp.float32)
    scale = lax.rsqrt(jnp.mean(values * values, axis=-1, keepdims=True) + 1e-05)
    normed = (values * scale).astype(jnp.bfloat16)
    normed_ref[...] = normed
    kv_ref[...] = dot(normed, kv_w_ref[...]).astype(jnp.bfloat16)


def butterfly_kernel(levels, mask_ref, *refs):
    (normed_ref, hidden_ref, q_w_ref, out_w_ref), refs = refs[:4], refs[4:]
    block_refs, refs = refs[: levels + 1], refs[levels + 1 :]
    out_ref, keys_ref, values_ref, q_ref, attended_ref = refs
    rows = normed_ref.shape[0]
    step = LANES
    q_ref[...] = dot(normed_ref[...], q_w_ref[...]).astype(jnp.bfloat16)
    for n, block in enumerate(block_refs):
        spread_keyvals(block[...], keys_ref, values_ref, n * rows)
    kv_heads = keys_ref.shape[0]
    pairs = q_ref.shape[1] // LANES
    shut = [None] + [jnp.where(mask_ref[0, level] == 1, 0.0, -LOW) for level in range(levels)]
    for pair in range(pairs):
        g = pair * kv_heads // pairs
        for part in range(rows // step):
            first = part * step
            q = q_ref[pl.ds(first, step), pair * LANES : (pair + 1) * LANES]
            total = None
            for s in range(2):
                scores = dot_t(q, keys_ref[g, s])
                top = None
                for n in range(levels + 1):
                    tiles = [
                        scores[:, n * rows + c : n * rows + c + LANES] for c in range(0, rows, LANES)
                    ]
                    one = functools.reduce(jnp.maximum, tiles)
                    if n:
                        one = one - shut[n]
                    top = one if top is None else jnp.maximum(top, one)
                top = jnp.max(top, axis=1, keepdims=True)
                weights = []
                for n in range(levels + 1):
                    base = top + shut[n] if n else top
                    weights.append(
                        jnp.exp2((scores[:, n * rows : (n + 1) * rows] - base) * SCALE).astype(
                            jnp.bfloat16
                        )
                    )
                mix = dot(jnp.concatenate(weights, axis=1), values_ref[g, s])
                total = mix if total is None else total + mix
            attended_ref[pl.ds(first, step), pair * LANES : (pair + 1) * LANES] = (
                total[:, :LANES] / total[:, LANES:]
            ).astype(jnp.bfloat16)
    out_ref[...] = (
        dot(attended_ref[...], out_w_ref[...]) + hidden_ref[...].astype(jnp.float32)
    ).astype(jnp.bfloat16)


def shards(
    residual,
    layer_queries,
    layer_keyvals,
    head_window_extent,
    block_mask,
    first_out,
    second_query,
    second_keyval,
    second_out,
):
    rows, width = residual.shape
    q_width = layer_queries.shape[1]
    kv_width = layer_keyvals.shape[1]
    kv_heads = kv_width // (2 * HEAD_SIZE)
    count = lax.axis_size("seq")
    levels = count.bit_length() - 1
    bf16 = jnp.bfloat16
    vmem = pl.BlockSpec(memory_space=pltpu.VMEM)
    smem = pl.BlockSpec(memory_space=pltpu.SMEM)
    hbm = pl.BlockSpec(memory_space=pl.ANY)

    from_left = lax.ppermute(layer_keyvals[-WIN:], "seq", [(i, i + 1) for i in range(count - 1)])
    from_right = lax.ppermute(layer_keyvals[:WIN], "seq", [(i + 1, i) for i in range(count - 1)])
    keys = rows + 2 * WIN
    hidden, normed, keyvals = pl.pallas_call(
        window_kernel,
        out_shape=[
            jax.ShapeDtypeStruct((rows, width), bf16),
            jax.ShapeDtypeStruct((rows, width), bf16),
            jax.ShapeDtypeStruct((rows, kv_width), bf16),
        ],
        in_specs=[smem, vmem, vmem, vmem, vmem, hbm, hbm, hbm],
        out_specs=[vmem] * 3,
        scratch_shapes=[
            pltpu.VMEM((kv_heads, 2, keys, LANES), bf16),
            pltpu.VMEM((kv_heads, 2, keys, 2 * LANES), bf16),
            pltpu.VMEM((rows, q_width), bf16),
            pltpu.VMEM(residual.shape, bf16),
            pltpu.VMEM(first_out.shape, bf16),
            pltpu.VMEM(second_keyval.shape, bf16),
            pltpu.SemaphoreType.DMA((3,)),
        ],
        compiler_params=pltpu.CompilerParams(vmem_limit_bytes=24 * 2**20),
        name="window",
    )(
        head_window_extent,
        layer_queries,
        from_left,
        layer_keyvals,
        from_right,
        residual,
        first_out,
        second_keyval,
    )

    others = [None] * levels
    for level in reversed(range(levels)):
        route = [(i, i ^ (1 << level)) for i in range(count)]
        others[level] = lax.ppermute(keyvals, "seq", route)
    keys = rows * (levels + 1)
    return pl.pallas_call(
        functools.partial(butterfly_kernel, levels),
        out_shape=jax.ShapeDtypeStruct((rows, width), bf16),
        in_specs=[smem] + [vmem] * (5 + levels),
        out_specs=vmem,
        scratch_shapes=[
            pltpu.VMEM((kv_heads, 2, keys, LANES), bf16),
            pltpu.VMEM((kv_heads, 2, keys, 2 * LANES), bf16),
            pltpu.VMEM((rows, q_width), bf16),
            pltpu.VMEM((rows, q_width), bf16),
        ],
        compiler_params=pltpu.CompilerParams(vmem_limit_bytes=24 * 2**20),
        name="butterfly",
    )(block_mask, normed, hidden, second_query, second_out, keyvals, *others)


def solution(mesh):
    tokens = P(("groups", "seq"), None)
    placed = (tokens, tokens, tokens, P(), P("seq", None), P(), P(), P(), P())
    return jax.shard_map(shards, mesh=mesh, in_specs=placed, out_specs=tokens, check_vma=False)
```

```python
import functools
import math

import jax
import jax.numpy as jnp
from jax import lax
from jax.experimental import pallas as pl
from jax.experimental.pallas import tpu as pltpu
from jax.sharding import PartitionSpec as P

HEAD_SIZE = 64
WIN = 256
LANES = 128
LOW = -1e30
SCALE = HEAD_SIZE**-0.5 * math.log2(math.e)
VMEM_LIMIT = 20 * 2**20


def dot(a, b):
    return jnp.dot(a, b, preferred_element_type=jnp.float32)


def dot_t(a, b):
    return lax.dot_general(a, b, (((1,), (1,)), ((), ())), preferred_element_type=jnp.float32)


def start_copies(pairs, sems):
    copies = [pltpu.make_async_copy(src, dst, sems.at[n]) for n, (src, dst) in enumerate(pairs)]
    for copy in copies:
        copy.start()
    return copies


def spread_keyvals(keyvals, keys_ref, values_ref, first):
    rows = keyvals.shape[0]
    kv_heads = keyvals.shape[1] // (2 * HEAD_SIZE)
    low = lax.broadcasted_iota(jnp.int32, (rows, LANES), 1) < HEAD_SIZE
    zero = jnp.zeros((rows, LANES), jnp.bfloat16)
    one = jnp.ones((rows, LANES), jnp.bfloat16)
    spot = pl.ds(first, rows)
    per_tile = LANES // HEAD_SIZE
    for g in range(kv_heads):
        tile, at = divmod(g, per_tile)
        k = keyvals[:, tile * LANES : (tile + 1) * LANES]
        v_first = kv_heads * HEAD_SIZE + tile * LANES
        v = keyvals[:, v_first : v_first + LANES]
        k_other = jnp.concatenate([k[:, HEAD_SIZE:], k[:, :HEAD_SIZE]], axis=1)
        v_other = jnp.concatenate([v[:, HEAD_SIZE:], v[:, :HEAD_SIZE]], axis=1)
        for s in range(2):
            here = low if s == 0 else jnp.logical_not(low)
            keys_ref[g, s, spot, :] = jnp.where(here, k if at == s else k_other, zero)
            values_ref[g, s, spot, :LANES] = jnp.where(here, v if at == s else v_other, zero)
            values_ref[g, s, spot, LANES:] = jnp.where(here, one, zero)


def attend(q_ref, keys_ref, values_ref, ranges, mask, prior, sink):
    kv_heads = keys_ref.shape[0]
    pairs = q_ref.shape[1] // LANES
    low = lax.broadcasted_iota(jnp.int32, (LANES, LANES), 1) < HEAD_SIZE
    for pair in range(pairs):
        g = pair * kv_heads // pairs
        for part, (first, span) in enumerate(ranges):
            here = pl.ds(part * LANES, LANES)
            q = q_ref[here, pair * LANES : (pair + 1) * LANES]
            total, tops, scales = None, [], []
            for s in range(2):
                scores = dot_t(q, keys_ref[g, s, pl.ds(first, span), :])
                tiles = [scores[:, c : c + LANES] for c in range(0, span, LANES)]
                tiles, tile_tops, bases = mask(pair, s, part, tiles)
                top = jnp.max(functools.reduce(jnp.maximum, tile_tops), axis=1, keepdims=True)
                top = jnp.broadcast_to(top, (LANES, LANES))
                if prior is not None:
                    old = prior[1][2 * pair + s, here, :]
                    top = jnp.maximum(top, old)
                    scales.append(jnp.exp2((old - top) * SCALE))
                weights = jnp.concatenate(
                    [
                        jnp.exp2((tile - (top if base is None else top + base)) * SCALE).astype(
                            jnp.bfloat16
                        )
                        for tile, base in zip(tiles, bases)
                    ],
                    axis=1,
                )
                mix = dot(weights, values_ref[g, s, pl.ds(first, span), :])
                total = mix if total is None else total + mix
                tops.append(top)
            sums = [total[:, :LANES], total[:, LANES:]]
            if prior is not None:
                scale = jnp.where(low, scales[0], scales[1])
                for n in range(2):
                    sums[n] = sums[n] + prior[0][n, here, pair * LANES : (pair + 1) * LANES] * scale
            sink(pair, part, sums, tops)


def keep_state(sums_ref, tops_ref):
    def sink(pair, part, sums, tops):
        here = pl.ds(part * LANES, LANES)
        for n in range(2):
            sums_ref[n, here, pair * LANES : (pair + 1) * LANES] = sums[n]
            tops_ref[2 * pair + n, here, :] = tops[n]

    return sink


def keep_heads(attended_ref):
    def sink(pair, part, sums, tops):
        attended_ref[pl.ds(part * LANES, LANES), pair * LANES : (pair + 1) * LANES] = (
            sums[0] / sums[1]
        ).astype(jnp.bfloat16)

    return sink


def window_mask(extent_ref, places, valid):
    row = lax.broadcasted_iota(jnp.int32, (LANES, LANES), 0)
    col = lax.broadcasted_iota(jnp.int32, (LANES, LANES), 1)
    gap = row - col

    def mask(pair, s, part, tiles):
        extent = extent_ref[2 * pair + s]
        out = []
        for tile, (ahead, side) in zip(tiles, places[part]):
            reach = extent if side is None else jnp.where(valid[side], extent, -1)
            if ahead < 0:
                seen = gap <= reach + ahead
            elif ahead > 0:
                seen = gap >= ahead - reach
            else:
                seen = jnp.abs(gap) <= reach
            out.append(jnp.where(seen, tile, LOW))
        return out, out, [None] * len(out)

    return mask


def own_window_kernel(
    extent_hbm, q_hbm, own_hbm, q_ref, sums_ref, tops_ref, extent_ref, own_ref, keys_ref, values_ref, sems
):
    copies = start_copies(((own_hbm, own_ref), (q_hbm, q_ref), (extent_hbm, extent_ref)), sems)
    rows = own_ref.shape[0]
    copies[0].wait()
    spread_keyvals(own_ref[...], keys_ref, values_ref, 0)
    for copy in copies[1:]:
        copy.wait()
    ranges, places = [], []
    for first in range(0, rows, LANES):
        near = [k for k in range(0, rows, LANES) if abs(k - first) < WIN + LANES]
        ranges.append((near[0], len(near) * LANES))
        places.append([(k - first, None) for k in near])
    attend(
        q_ref,
        keys_ref,
        values_ref,
        ranges,
        window_mask(extent_ref, places, None),
        None,
        keep_state(sums_ref, tops_ref),
    )


def halo_window_kernel(
    extent_hbm,
    q_ref,
    even_ref,
    odd_ref,
    sums_ref,
    tops_ref,
    residual_hbm,
    out_w_hbm,
    kv_w_hbm,
    hidden_ref,
    normed_ref,
    kv_ref,
    extent_ref,
    keys_ref,
    values_ref,
    attended_ref,
    residual_ref,
    out_w_ref,
    kv_w_ref,
    sems,
):
    copies = start_copies(
        (
            (extent_hbm, extent_ref),
            (out_w_hbm, out_w_ref),
            (residual_hbm, residual_ref),
            (kv_w_hbm, kv_w_ref),
        ),
        sems,
    )
    rows = q_ref.shape[0]
    me = lax.axis_index("seq")
    valid = (me > 0, me < lax.axis_size("seq") - 1)
    left_is_even = lax.rem(me, 2)
    for block, after in ((even_ref, 1 - left_is_even), (odd_ref, left_is_even)):
        spread_keyvals(block[...], keys_ref, values_ref, pl.multiple_of(after * WIN, WIN))
    copies[0].wait()
    ranges, places = [], []
    for first in range(0, rows, LANES):
        left = [(k - first, 0) for k in range(-WIN, 0, LANES) if first - k < WIN + LANES]
        right = [
            (k - first, 1) for k in range(rows, rows + WIN, LANES) if k - first < WIN + LANES
        ]
        places.append(left + right)
        ranges.append((WIN - len(left) * LANES, len(left + right) * LANES))
    attend(
        q_ref,
        keys_ref,
        values_ref,
        ranges,
        window_mask(extent_ref, places, valid),
        (sums_ref, tops_ref),
        keep_heads(attended_ref),
    )
    for copy in copies[1:]:
        copy.wait()
    hidden = (
        dot(attended_ref[...], out_w_ref[...]) + residual_ref[...].astype(jnp.float32)
    ).astype(jnp.bfloat16)
    hidden_ref[...] = hidden
    values = hidden.astype(jnp.float32)
    scale = lax.rsqrt(jnp.mean(values * values, axis=-1, keepdims=True) + 1e-05)
    normed = (values * scale).astype(jnp.bfloat16)
    normed_ref[...] = normed
    kv_ref[...] = dot(normed, kv_w_ref[...]).astype(jnp.bfloat16)


def open_mask(tiles_per_block, shut):
    def mask(pair, s, part, tiles):
        tops, bases = [], []
        for n, one in enumerate(shut):
            block = tiles[n * tiles_per_block : (n + 1) * tiles_per_block]
            top = functools.reduce(jnp.maximum, block)
            tops.append(top if one is None else top - one)
            bases += [one] * tiles_per_block
        return tiles, tops, bases

    return mask


def own_butterfly_kernel(
    levels,
    mask_hbm,
    normed_ref,
    q_w_ref,
    own_ref,
    q_ref,
    sums_ref,
    tops_ref,
    shut_ref,
    mask_ref,
    keys_ref,
    values_ref,
    sems,
):
    copies = start_copies(((mask_hbm, mask_ref),), sems)
    rows = normed_ref.shape[0]
    q_ref[...] = dot(normed_ref[...], q_w_ref[...]).astype(jnp.bfloat16)
    spread_keyvals(own_ref[...], keys_ref, values_ref, 0)
    attend(
        q_ref,
        keys_ref,
        values_ref,
        [(0, rows)] * (rows // LANES),
        open_mask(rows // LANES, [None]),
        None,
        keep_state(sums_ref, tops_ref),
    )
    copies[0].wait()
    for level in range(levels):
        shut = jnp.where(mask_ref[0, level] == 1, 0.0, -LOW)
        shut_ref[level] = jnp.full(shut_ref.shape[1:], shut, jnp.float32)


def more_butterfly_kernel(levels, last, *refs):
    blocks, refs = refs[: len(levels)], refs[len(levels) :]
    (shut_ref, q_ref, sums_ref, tops_ref), refs = refs[:4], refs[4:]
    rows = q_ref.shape[0]
    if last:
        hidden_ref, out_w_ref, out_ref, keys_ref, values_ref, attended_ref = refs
        sink = keep_heads(attended_ref)
    else:
        sums_out_ref, tops_out_ref, keys_ref, values_ref = refs
        sink = keep_state(sums_out_ref, tops_out_ref)
    for n, block in enumerate(blocks):
        spread_keyvals(block[...], keys_ref, values_ref, n * rows)
    shut = [jnp.broadcast_to(shut_ref[level, :1, :], (LANES, LANES)) for level in levels]
    attend(
        q_ref,
        keys_ref,
        values_ref,
        [(0, rows * len(levels))] * (rows // LANES),
        open_mask(rows // LANES, shut),
        (sums_ref, tops_ref),
        sink,
    )
    if last:
        out_ref[...] = (
            dot(attended_ref[...], out_w_ref[...]) + hidden_ref[...].astype(jnp.float32)
        ).astype(jnp.bfloat16)


def exchange_edges(block, parity):
    groups, count = lax.axis_size("groups"), lax.axis_size("seq")
    rows = block.shape[0]
    if rows > WIN:
        first = jnp.where(lax.rem(lax.axis_index("seq"), 2) == parity, rows - WIN, 0)
        block = lax.dynamic_slice_in_dim(block, first, WIN, 0)
    route = []
    for group in range(groups):
        for i in range(count):
            other, to = group, i + 1 if i % 2 == parity else i - 1
            if not 0 <= to < count:
                other, to = (group ^ 1 if group ^ 1 < groups else group), i
            route.append((group * count + i, other * count + to))
    return lax.ppermute(block, ("groups", "seq"), route)


def shards(
    residual,
    layer_queries,
    layer_keyvals,
    head_window_extent,
    block_mask,
    first_out,
    second_query,
    second_keyval,
    second_out,
):
    rows, width = residual.shape
    q_width = layer_queries.shape[1]
    kv_width = layer_keyvals.shape[1]
    kv_heads = kv_width // (2 * HEAD_SIZE)
    heads = q_width // HEAD_SIZE
    count = lax.axis_size("seq")
    level_count = count.bit_length() - 1
    bf16, f32 = jnp.bfloat16, jnp.float32
    vmem = pl.BlockSpec(memory_space=pltpu.VMEM)
    hbm = pl.BlockSpec(memory_space=pltpu.HBM)
    state = [
        jax.ShapeDtypeStruct((2, rows, q_width), f32),
        jax.ShapeDtypeStruct((heads, rows, LANES), f32),
    ]
    queries = jax.ShapeDtypeStruct((rows, q_width), bf16)
    wide = jax.ShapeDtypeStruct((rows, width), bf16)

    def call(kernel, name, in_specs, out_shape, scratch, key_rows, extra_macs, args):
        macs = 4 * rows * heads * HEAD_SIZE * key_rows + extra_macs
        spread = [
            pltpu.VMEM((kv_heads, 2, key_rows, LANES), bf16),
            pltpu.VMEM((kv_heads, 2, key_rows, 2 * LANES), bf16),
        ]
        at = next((n for n, one in enumerate(scratch) if one is None))
        return pl.pallas_call(
            kernel,
            out_shape=out_shape,
            in_specs=in_specs,
            out_specs=jax.tree.map(lambda _: vmem, out_shape),
            scratch_shapes=scratch[:at] + spread + scratch[at + 1 :],
            compiler_params=pltpu.CompilerParams(vmem_limit_bytes=VMEM_LIMIT),
            cost_estimate=pl.CostEstimate(
                flops=16 * macs, bytes_accessed=2**21, transcendentals=rows * heads * key_rows
            ),
            name=name,
        )(*args)

    even, odd = (exchange_edges(layer_keyvals, parity) for parity in range(2))
    q_here, sums, tops = call(
        own_window_kernel,
        "own_window",
        [hbm] * 3,
        [queries] + state,
        [
            pltpu.SMEM(head_window_extent.shape, jnp.int32),
            pltpu.VMEM(layer_keyvals.shape, bf16),
            None,
            pltpu.SemaphoreType.DMA((3,)),
        ],
        rows,
        0,
        (head_window_extent, layer_queries, layer_keyvals),
    )
    hidden, normed, keyvals = call(
        halo_window_kernel,
        "halo_window",
        [hbm] + [vmem] * 5 + [hbm] * 3,
        [wide, wide, jax.ShapeDtypeStruct((rows, kv_width), bf16)],
        [
            pltpu.SMEM(head_window_extent.shape, jnp.int32),
            None,
            pltpu.VMEM((rows, q_width), bf16),
            pltpu.VMEM(residual.shape, bf16),
            pltpu.VMEM(first_out.shape, bf16),
            pltpu.VMEM(second_keyval.shape, bf16),
            pltpu.SemaphoreType.DMA((4,)),
        ],
        2 * WIN,
        rows * width * (q_width + kv_width),
        (
            head_window_extent,
            q_here,
            even,
            odd,
            sums,
            tops,
            residual,
            first_out,
            second_keyval,
        ),
    )

    others = [None] * level_count
    for level in reversed(range(level_count)):
        route = [(i, i ^ (1 << level)) for i in range(count)]
        others[level] = lax.ppermute(keyvals, "seq", route)
    queries_two, sums, tops, shut = call(
        functools.partial(own_butterfly_kernel, level_count),
        "own_butterfly",
        [hbm] + [vmem] * 3,
        [queries] + state + [jax.ShapeDtypeStruct((level_count, 8, LANES), f32)],
        [pltpu.SMEM(block_mask.shape, jnp.int32), None, pltpu.SemaphoreType.DMA((1,))],
        rows,
        rows * width * q_width,
        (block_mask, normed, second_query, keyvals),
    )
    cut = (level_count + 1) // 2
    groups = [list(reversed(range(cut))), list(reversed(range(cut, level_count)))]
    for levels in groups[:-1]:
        sums, tops = call(
            functools.partial(more_butterfly_kernel, levels, False),
            "near_butterfly",
            [vmem] * (4 + len(levels)),
            state,
            [None],
            rows * len(levels),
            0,
            (*[others[level] for level in levels], shut, queries_two, sums, tops),
        )
    levels = groups[-1]
    return call(
        functools.partial(more_butterfly_kernel, levels, True),
        "far_butterfly",
        [vmem] * (6 + len(levels)),
        wide,
        [None, pltpu.VMEM((rows, q_width), bf16)],
        rows * len(levels),
        rows * width * q_width,
        (*[others[level] for level in levels], shut, queries_two, sums, tops, hidden, second_out),
    )


def solution(mesh):
    tokens = P(("groups", "seq"), None)
    placed = (tokens, tokens, tokens, P(), P("seq", None), P(), P(), P(), P())
    return jax.shard_map(shards, mesh=mesh, in_specs=placed, out_specs=tokens, check_vma=False)
```

```python
import functools
import math

import jax
import jax.numpy as jnp
from jax import lax
from jax.experimental import pallas as pl
from jax.experimental.pallas import tpu as pltpu
from jax.sharding import PartitionSpec as P

HEAD_SIZE = 64
WIN = 256
LANES = 128
LOW = -1e30
SCALE = HEAD_SIZE**-0.5 * math.log2(math.e)
VMEM_LIMIT = 20 * 2**20
ROWS = 256


def dot(a, b):
    return jnp.dot(a, b, preferred_element_type=jnp.float32)


def dot_t(a, b):
    return lax.dot_general(a, b, (((1,), (1,)), ((), ())), preferred_element_type=jnp.float32)


def swap_halves(tile):
    return jnp.concatenate([tile[:, HEAD_SIZE:], tile[:, :HEAD_SIZE]], axis=1)


def low_half(rows):
    return lax.broadcasted_iota(jnp.int32, (rows, LANES), 1) < HEAD_SIZE


def spread_queries(queries, kv_heads, spread_ref):
    rows, width = queries.shape
    heads = width // HEAD_SIZE
    low = low_half(rows)
    for head in range(heads):
        at, want = head % 2, head * kv_heads // heads % 2
        tile = queries[:, head // 2 * LANES : (head // 2 + 1) * LANES]
        if at != want:
            tile = swap_halves(tile)
        here = low if want == 0 else jnp.logical_not(low)
        spread_ref[head] = jnp.where(here, tile, jnp.zeros_like(tile))


def spread_values(keyvals, values_ref, first, shown=None):
    rows, width = keyvals.shape
    kv_heads = width // (2 * HEAD_SIZE)
    low = low_half(rows)
    for g in range(kv_heads):
        begin = width // 2 + g // 2 * LANES
        tile = keyvals[:, begin : begin + LANES]
        other = swap_halves(tile)
        for s in range(2):
            here = low if s == 0 else jnp.logical_not(low)
            out = jnp.where(here, tile if g % 2 == s else other, jnp.ones_like(tile))
            if shown is not None:
                out = out * shown
            values_ref[g, s, pl.ds(first, rows), :] = out


def attend(q_ref, key_refs, values_ref, parts, mask, prior, sink):
    heads = q_ref.shape[0]
    kv_heads = values_ref.shape[0]
    steps = [
        (g, s, [h for h in range(heads) if h * kv_heads // heads == g and h % 2 == s], part)
        for g in range(kv_heads)
        for s in range(2)
        for part in range(len(parts))
    ]

    def score(g, s, mine, part):
        row, rows, key, span = parts[part]
        q = jnp.concatenate([q_ref[h, pl.ds(row, rows), :] for h in mine], axis=0)
        tiles, at = [], 0
        for ref in key_refs:
            begin, end = max(key - at, 0), min(key + span - at, ref.shape[0])
            if begin < end:
                keys = ref[pl.ds(begin, end - begin), pl.ds(g // 2 * LANES, LANES)]
                scores = dot_t(q, keys)
                tiles += [scores[:, c : c + LANES] for c in range(0, end - begin, LANES)]
            at += ref.shape[0]
        return tiles

    def mix(g, s, mine, part, tiles):
        row, rows, key, span = parts[part]
        here = pl.ds(row, rows)
        weights, tops, scales = [], [], []
        for n, h in enumerate(mine):
            some = mask(h, part, [tile[n * rows : (n + 1) * rows] for tile in tiles])
            top = jnp.max(functools.reduce(jnp.maximum, some), axis=1, keepdims=True)
            top = jnp.broadcast_to(top, (rows, LANES))
            if prior is not None:
                old = prior[1][h, here, :]
                top = jnp.maximum(top, old)
                scales.append(jnp.exp2((old - top) * SCALE))
            tops.append(top)
            weights.append(
                jnp.concatenate(
                    [jnp.exp2((tile - top) * SCALE).astype(jnp.bfloat16) for tile in some], axis=1
                )
            )
        sums = dot(jnp.concatenate(weights, axis=0), values_ref[g, s, pl.ds(key, span), :])
        for n, h in enumerate(mine):
            one = sums[n * rows : (n + 1) * rows]
            if prior is not None:
                one = one + prior[0][h, here, :] * scales[n]
            sink(h, here, one, tops[n])

    tiles = score(*steps[0])
    for n, step in enumerate(steps):
        ahead = score(*steps[n + 1]) if n + 1 < len(steps) else None
        mix(*step, tiles)
        tiles = ahead


def keep_state(sums_ref, tops_ref):
    def sink(head, here, sums, top):
        sums_ref[head, here, :] = sums
        tops_ref[head, here, :] = top

    return sink


def keep_sums(sums_ref):
    def sink(head, here, sums, top):
        sums_ref[head, here, :] = sums

    return sink


def divide_pairs(sums_ref):
    heads, rows, _ = sums_ref.shape
    low = low_half(rows)
    out = []
    for head in range(0, heads, 2):
        even, odd = sums_ref[head], sums_ref[head + 1]
        total = swap_halves(jnp.where(low, odd, even))
        out.append((jnp.where(low, even, odd) / total).astype(jnp.bfloat16))
    return jnp.concatenate(out, axis=1)


def window_mask(extent_ref, places, valid):
    def mask(head, part, tiles):
        extent = extent_ref[head]
        shape = tiles[0].shape
        gap = lax.broadcasted_iota(jnp.int32, shape, 0) - lax.broadcasted_iota(jnp.int32, shape, 1)
        out = []
        for tile, (ahead, side) in zip(tiles, places[part]):
            reach = extent if side is None else jnp.where(valid[side], extent, -1)
            if ahead <= -shape[1]:
                seen = gap <= reach + ahead
            elif ahead >= shape[0]:
                seen = gap >= ahead - reach
            else:
                seen = jnp.abs(gap - ahead) <= reach
            out.append(jnp.where(seen, tile, LOW))
        return out

    return mask


def own_window_kernel(
    extent_ref, queries_ref, own_ref, q_ref, sums_ref, tops_ref, values_ref
):
    rows = own_ref.shape[0]
    kv_heads = values_ref.shape[0]
    spread_queries(queries_ref[...], kv_heads, q_ref)
    spread_values(own_ref[...], values_ref, 0)
    step = min(rows, ROWS)
    parts, places = [], []
    for row in range(0, rows, step):
        near = [k for k in range(0, rows, LANES) if row - k < WIN + LANES and k - row < WIN + step]
        parts.append((row, step, near[0], len(near) * LANES))
        places.append([(k - row, None) for k in near])
    attend(
        q_ref,
        [own_ref],
        values_ref,
        parts,
        window_mask(extent_ref, places, None),
        None,
        keep_state(sums_ref, tops_ref),
    )


def halo_window_kernel(
    extent_ref,
    q_ref,
    even_ref,
    odd_ref,
    sums_ref,
    tops_ref,
    residual_ref,
    out_w_ref,
    kv_w_ref,
    hidden_ref,
    normed_ref,
    kv_ref,
    values_ref,
    keys_ref,
    all_sums_ref,
):
    rows = q_ref.shape[1]
    key_width = even_ref.shape[1] // 2
    me = lax.axis_index("seq")
    valid = (me > 0, me < lax.axis_size("seq") - 1)
    left_is_even = lax.rem(me, 2)
    for block, after in ((even_ref, 1 - left_is_even), (odd_ref, left_is_even)):
        first = pl.multiple_of(after * WIN, WIN)
        keys_ref[pl.ds(first, WIN), :] = block[:, :key_width]
        spread_values(block[...], values_ref, first)
    step = LANES
    parts, places = [], []
    for row in range(0, rows, step):
        left = [(k - row, 0) for k in range(-WIN, 0, LANES) if row - k < WIN + LANES]
        right = [(k - row, 1) for k in range(rows, rows + WIN, LANES) if k - row < WIN + step]
        places.append(left + right)
        parts.append((row, step, WIN - len(left) * LANES, len(left + right) * LANES))
    attend(
        q_ref,
        [keys_ref],
        values_ref,
        parts,
        window_mask(extent_ref, places, valid),
        (sums_ref, tops_ref),
        keep_sums(all_sums_ref),
    )
    hidden = (
        dot(divide_pairs(all_sums_ref), out_w_ref[...]) + residual_ref[...].astype(jnp.float32)
    ).astype(jnp.bfloat16)
    hidden_ref[...] = hidden
    values = hidden.astype(jnp.float32)
    scale = lax.rsqrt(jnp.mean(values * values, axis=-1, keepdims=True) + 1e-05)
    normed = (values * scale).astype(jnp.bfloat16)
    normed_ref[...] = normed
    kv_ref[...] = dot(normed, kv_w_ref[...]).astype(jnp.bfloat16)


def all_seen(head, part, tiles):
    return tiles


def own_butterfly_kernel(
    levels,
    mask_ref,
    normed_ref,
    q_w_ref,
    own_ref,
    q_ref,
    sums_ref,
    tops_ref,
    shown_ref,
    values_ref,
):
    rows = normed_ref.shape[0]
    kv_heads = values_ref.shape[0]
    for level in range(levels):
        shown_ref[level] = jnp.full(
            shown_ref.shape[1:], jnp.where(mask_ref[0, level] == 1, 1.0, 0.0), jnp.bfloat16
        )
    spread_queries(
        dot(normed_ref[...], q_w_ref[...]).astype(jnp.bfloat16), kv_heads, q_ref
    )
    spread_values(own_ref[...], values_ref, 0)
    step = min(rows, ROWS)
    attend(
        q_ref,
        [own_ref],
        values_ref,
        [(row, step, 0, rows) for row in range(0, rows, step)],
        all_seen,
        None,
        keep_state(sums_ref, tops_ref),
    )


def more_butterfly_kernel(levels, last, *refs):
    blocks, refs = refs[: len(levels)], refs[len(levels) :]
    (shown_ref, own_ref, q_ref, sums_ref, tops_ref), refs = refs[:5], refs[5:]
    rows = q_ref.shape[1]
    if last:
        hidden_ref, out_w_ref, out_ref, values_ref, keys_ref, all_sums_ref = refs
        sink = keep_sums(all_sums_ref)
    else:
        sums_out_ref, tops_out_ref, values_ref, keys_ref = refs
        sink = keep_state(sums_out_ref, tops_out_ref)
    key_width = own_ref.shape[1] // 2
    for n, (level, block) in enumerate(zip(levels, blocks)):
        spot = pl.ds(n * rows, rows)
        shown = shown_ref[level, :1, :]
        for c in range(0, key_width, LANES):
            keys = block[:, c : c + LANES]
            here = jnp.broadcast_to(shown, keys.shape) > 0
            keys_ref[spot, c : c + LANES] = jnp.where(here, keys, own_ref[:, c : c + LANES])
        spread_values(block[...], values_ref, n * rows, shown)
    step = min(rows, ROWS)
    attend(
        q_ref,
        [keys_ref],
        values_ref,
        [(row, step, 0, rows * len(levels)) for row in range(0, rows, step)],
        all_seen,
        (sums_ref, tops_ref),
        sink,
    )
    if last:
        out_ref[...] = (
            dot(divide_pairs(all_sums_ref), out_w_ref[...]) + hidden_ref[...].astype(jnp.float32)
        ).astype(jnp.bfloat16)


def exchange_edges(block, parity):
    groups, count = lax.axis_size("groups"), lax.axis_size("seq")
    rows = block.shape[0]
    if rows > WIN:
        first = jnp.where(lax.rem(lax.axis_index("seq"), 2) == parity, rows - WIN, 0)
        block = lax.dynamic_slice_in_dim(block, first, WIN, 0)
    route = []
    for group in range(groups):
        for i in range(count):
            other, to = group, i + 1 if i % 2 == parity else i - 1
            if not 0 <= to < count:
                other, to = (group ^ 1 if group ^ 1 < groups else group), i
            route.append((group * count + i, other * count + to))
    return lax.ppermute(block, ("groups", "seq"), route)


def shards(
    residual,
    layer_queries,
    layer_keyvals,
    head_window_extent,
    block_mask,
    first_out,
    second_query,
    second_keyval,
    second_out,
):
    rows, width = residual.shape
    q_width = layer_queries.shape[1]
    kv_width = layer_keyvals.shape[1]
    kv_heads = kv_width // (2 * HEAD_SIZE)
    heads = q_width // HEAD_SIZE
    count = lax.axis_size("seq")
    level_count = count.bit_length() - 1
    bf16, f32 = jnp.bfloat16, jnp.float32
    vmem = pl.BlockSpec(memory_space=pltpu.VMEM)
    smem = pl.BlockSpec(memory_space=pltpu.SMEM)
    state = [jax.ShapeDtypeStruct((heads, rows, LANES), f32)] * 2
    queries = jax.ShapeDtypeStruct((heads, rows, LANES), bf16)
    wide = jax.ShapeDtypeStruct((rows, width), bf16)
    all_sums = pltpu.VMEM((heads, rows, LANES), f32)

    def call(kernel, name, in_specs, out_shape, scratch, key_rows, extra_macs, args):
        macs = 4 * rows * heads * HEAD_SIZE * key_rows + extra_macs
        values = pltpu.VMEM((kv_heads, 2, key_rows, LANES), bf16)
        return pl.pallas_call(
            kernel,
            out_shape=out_shape,
            in_specs=in_specs,
            out_specs=jax.tree.map(lambda _: vmem, out_shape),
            scratch_shapes=[values] + scratch,
            compiler_params=pltpu.CompilerParams(vmem_limit_bytes=VMEM_LIMIT),
            cost_estimate=pl.CostEstimate(
                flops=16 * macs, bytes_accessed=2**21, transcendentals=rows * heads * key_rows
            ),
            name=name,
        )(*args)

    even, odd = (exchange_edges(layer_keyvals, parity) for parity in range(2))
    q_here, sums, tops = call(
        own_window_kernel,
        "own_window",
        [smem, vmem, vmem],
        [queries] + state,
        [],
        rows,
        0,
        (head_window_extent, layer_queries, layer_keyvals),
    )
    hidden, normed, keyvals = call(
        halo_window_kernel,
        "halo_window",
        [smem] + [vmem] * 8,
        [wide, wide, jax.ShapeDtypeStruct((rows, kv_width), bf16)],
        [pltpu.VMEM((2 * WIN, kv_width // 2), bf16), all_sums],
        2 * WIN,
        rows * width * (q_width + kv_width),
        (
            head_window_extent,
            q_here,
            even,
            odd,
            sums,
            tops,
            residual,
            first_out,
            second_keyval,
        ),
    )

    others = [None] * level_count
    for level in reversed(range(level_count)):
        route = [(i, i ^ (1 << level)) for i in range(count)]
        others[level] = lax.ppermute(keyvals, "seq", route)
    queries_two, sums, tops, shown = call(
        functools.partial(own_butterfly_kernel, level_count),
        "own_butterfly",
        [smem] + [vmem] * 3,
        [queries] + state + [jax.ShapeDtypeStruct((level_count, 16, LANES), bf16)],
        [],
        rows,
        rows * width * q_width,
        (block_mask, normed, second_query, keyvals),
    )
    cut = (level_count + 1) // 2
    groups = [list(reversed(range(cut))), list(reversed(range(cut, level_count)))]


    def key_block(levels):
        return pltpu.VMEM((rows * len(levels), kv_width // 2), bf16)

    for levels in groups[:-1]:
        sums, tops = call(
            functools.partial(more_butterfly_kernel, levels, False),
            "near_butterfly",
            [vmem] * (5 + len(levels)),
            state,
            [key_block(levels)],
            rows * len(levels),
            0,
            (*[others[level] for level in levels], shown, keyvals, queries_two, sums, tops),
        )
    levels = groups[-1]
    return call(
        functools.partial(more_butterfly_kernel, levels, True),
        "far_butterfly",
        [vmem] * (7 + len(levels)),
        wide,
        [key_block(levels), all_sums],
        rows * len(levels),
        rows * width * q_width,
        (*[others[level] for level in levels], shown, keyvals, queries_two, sums, tops, hidden, second_out),
    )


def solution(mesh):
    tokens = P(("groups", "seq"), None)
    placed = (tokens, tokens, tokens, P(), P("seq", None), P(), P(), P(), P())
    return jax.shard_map(shards, mesh=mesh, in_specs=placed, out_specs=tokens, check_vma=False)
```

```python
import functools
import math

import jax
import jax.numpy as jnp
from jax import lax
from jax.experimental import pallas as pl
from jax.experimental.pallas import tpu as pltpu
from jax.sharding import PartitionSpec as P

HEAD_SIZE = 64
WIN = 256
LANES = 128
LOW = -1e30
SCALE = HEAD_SIZE**-0.5 * math.log2(math.e)
VMEM_LIMIT = 20 * 2**20
ROWS = 256


def dot(a, b):
    return jnp.dot(a, b, preferred_element_type=jnp.float32)


def dot_t(a, b):
    return lax.dot_general(a, b, (((1,), (1,)), ((), ())), preferred_element_type=jnp.float32)


def swap_halves(tile):
    return jnp.concatenate([tile[:, HEAD_SIZE:], tile[:, :HEAD_SIZE]], axis=1)


def low_half(rows):
    return lax.broadcasted_iota(jnp.int32, (rows, LANES), 1) < HEAD_SIZE


def splat(row, index, shape):
    lane = lax.broadcasted_iota(jnp.int32, row.shape, 1)
    one = jnp.sum(jnp.where(lane == index, row.astype(jnp.float32), 0.0), axis=1, keepdims=True)
    return jnp.broadcast_to(one, shape)


def spread_queries(queries, kv_heads, spread_ref):
    rows, width = queries.shape
    heads = width // HEAD_SIZE
    low = low_half(rows)
    for head in range(heads):
        at, want = head % 2, head * kv_heads // heads % 2
        tile = queries[:, head // 2 * LANES : (head // 2 + 1) * LANES]
        if at != want:
            tile = swap_halves(tile)
        here = low if want == 0 else jnp.logical_not(low)
        spread_ref[head] = jnp.where(here, tile, jnp.zeros_like(tile))


def spread_values(keyvals, values_ref, first, shown=None):
    rows, width = keyvals.shape
    kv_heads = width // (2 * HEAD_SIZE)
    low = low_half(rows)
    for g in range(kv_heads):
        begin = width // 2 + g // 2 * LANES
        tile = keyvals[:, begin : begin + LANES]
        other = swap_halves(tile)
        for s in range(2):
            here = low if s == 0 else jnp.logical_not(low)
            out = jnp.where(here, tile if g % 2 == s else other, jnp.ones_like(tile))
            if shown is not None:
                out = out * shown
            values_ref[g, s, pl.ds(first, rows), :] = out


def attend(q_ref, key_refs, values_ref, parts, mask, prior, sink):
    heads = q_ref.shape[0]
    kv_heads = values_ref.shape[0]
    steps = [
        (g, s, [h for h in range(heads) if h * kv_heads // heads == g and h % 2 == s], part)
        for g in range(kv_heads)
        for s in range(2)
        for part in range(len(parts))
    ]

    def score(g, s, mine, part):
        row, rows, key, span = parts[part]
        q = jnp.concatenate([q_ref[h, pl.ds(row, rows), :] for h in mine], axis=0)
        tiles, at = [], 0
        for ref in key_refs:
            begin, end = max(key - at, 0), min(key + span - at, ref.shape[0])
            if begin < end:
                keys = ref[pl.ds(begin, end - begin), pl.ds(g // 2 * LANES, LANES)]
                scores = dot_t(q, keys)
                tiles += [scores[:, c : c + LANES] for c in range(0, end - begin, LANES)]
            at += ref.shape[0]
        return tiles

    def mix(g, s, mine, part, tiles):
        row, rows, key, span = parts[part]
        here = pl.ds(row, rows)
        weights, tops, scales = [], [], []
        for n, h in enumerate(mine):
            some = mask(h, part, [tile[n * rows : (n + 1) * rows] for tile in tiles])
            top = jnp.max(functools.reduce(jnp.maximum, some), axis=1, keepdims=True)
            top = jnp.broadcast_to(top, (rows, LANES))
            if prior is not None:
                old = prior[1][h, here, :]
                top = jnp.maximum(top, old)
                scales.append(jnp.exp2((old - top) * SCALE))
            tops.append(top)
            weights.append(
                jnp.concatenate(
                    [jnp.exp2((tile - top) * SCALE).astype(jnp.bfloat16) for tile in some], axis=1
                )
            )
        sums = dot(jnp.concatenate(weights, axis=0), values_ref[g, s, pl.ds(key, span), :])
        for n, h in enumerate(mine):
            one = sums[n * rows : (n + 1) * rows]
            if prior is not None:
                one = one + prior[0][h, here, :] * scales[n]
            sink(h, here, one, tops[n])

    tiles = score(*steps[0])
    for n, step in enumerate(steps):
        ahead = score(*steps[n + 1]) if n + 1 < len(steps) else None
        mix(*step, tiles)
        tiles = ahead


def keep_state(sums_ref, tops_ref):
    def sink(head, here, sums, top):
        sums_ref[head, here, :] = sums
        tops_ref[head, here, :] = top

    return sink


def keep_sums(sums_ref):
    def sink(head, here, sums, top):
        sums_ref[head, here, :] = sums

    return sink


def divide_pairs(sums_ref):
    heads, rows, _ = sums_ref.shape
    low = low_half(rows)
    out = []
    for head in range(0, heads, 2):
        even, odd = sums_ref[head], sums_ref[head + 1]
        total = swap_halves(jnp.where(low, odd, even))
        out.append((jnp.where(low, even, odd) / total).astype(jnp.bfloat16))
    return jnp.concatenate(out, axis=1)


def window_mask(extents_ref, places, valid):
    def mask(head, part, tiles):
        extent = extents_ref[head, :1, :]
        shape = tiles[0].shape
        gap = lax.broadcasted_iota(jnp.int32, shape, 0) - lax.broadcasted_iota(jnp.int32, shape, 1)
        out = []
        for tile, (ahead, side) in zip(tiles, places[part]):
            reach = extent if side is None else jnp.where(valid[side], extent, -1)
            if ahead <= -shape[1]:
                seen = gap <= reach + ahead
            elif ahead >= shape[0]:
                seen = gap >= ahead - reach
            else:
                seen = jnp.abs(gap - ahead) <= reach
            out.append(jnp.where(seen, tile, LOW))
        return out

    return mask


def own_window_kernel(
    extent_ref, queries_ref, own_ref, extents_ref, q_ref, sums_ref, tops_ref, values_ref
):
    rows = own_ref.shape[0]
    for head in range(extents_ref.shape[0]):
        one = splat(extent_ref[...], head, extents_ref.shape[1:])
        extents_ref[head] = one.astype(jnp.int32)
    kv_heads = values_ref.shape[0]
    spread_queries(queries_ref[...], kv_heads, q_ref)
    spread_values(own_ref[...], values_ref, 0)
    step = min(rows, ROWS)
    parts, places = [], []
    for row in range(0, rows, step):
        near = [k for k in range(0, rows, LANES) if row - k < WIN + LANES and k - row < WIN + step]
        parts.append((row, step, near[0], len(near) * LANES))
        places.append([(k - row, None) for k in near])
    attend(
        q_ref,
        [own_ref],
        values_ref,
        parts,
        window_mask(extents_ref, places, None),
        None,
        keep_state(sums_ref, tops_ref),
    )


def halo_window_kernel(
    extents_ref,
    q_ref,
    even_ref,
    odd_ref,
    sums_ref,
    tops_ref,
    residual_ref,
    out_w_ref,
    kv_w_ref,
    hidden_ref,
    normed_ref,
    kv_ref,
    values_ref,
    keys_ref,
    all_sums_ref,
):
    rows = q_ref.shape[1]
    key_width = even_ref.shape[1] // 2
    me = lax.axis_index("seq")
    valid = (me > 0, me < lax.axis_size("seq") - 1)
    left_is_even = lax.rem(me, 2)
    for block, after in ((even_ref, 1 - left_is_even), (odd_ref, left_is_even)):
        first = pl.multiple_of(after * WIN, WIN)
        keys_ref[pl.ds(first, WIN), :] = block[:, :key_width]
        spread_values(block[...], values_ref, first)
    step = LANES
    parts, places = [], []
    for row in range(0, rows, step):
        left = [(k - row, 0) for k in range(-WIN, 0, LANES) if row - k < WIN + LANES]
        right = [(k - row, 1) for k in range(rows, rows + WIN, LANES) if k - row < WIN + step]
        places.append(left + right)
        parts.append((row, step, WIN - len(left) * LANES, len(left + right) * LANES))
    attend(
        q_ref,
        [keys_ref],
        values_ref,
        parts,
        window_mask(extents_ref, places, valid),
        (sums_ref, tops_ref),
        keep_sums(all_sums_ref),
    )
    hidden = (
        dot(divide_pairs(all_sums_ref), out_w_ref[...]) + residual_ref[...].astype(jnp.float32)
    ).astype(jnp.bfloat16)
    hidden_ref[...] = hidden
    values = hidden.astype(jnp.float32)
    scale = lax.rsqrt(jnp.mean(values * values, axis=-1, keepdims=True) + 1e-05)
    normed = (values * scale).astype(jnp.bfloat16)
    normed_ref[...] = normed
    kv_ref[...] = dot(normed, kv_w_ref[...]).astype(jnp.bfloat16)


def all_seen(head, part, tiles):
    return tiles


def own_butterfly_kernel(
    levels,
    mask_ref,
    normed_ref,
    q_w_ref,
    own_ref,
    q_ref,
    sums_ref,
    tops_ref,
    shown_ref,
    values_ref,
):
    rows = normed_ref.shape[0]
    kv_heads = values_ref.shape[0]
    for level in range(levels):
        one = splat(mask_ref[...], level, shown_ref.shape[1:])
        shown_ref[level] = jnp.where(one == 1.0, 1.0, 0.0).astype(jnp.bfloat16)
    spread_queries(
        dot(normed_ref[...], q_w_ref[...]).astype(jnp.bfloat16), kv_heads, q_ref
    )
    spread_values(own_ref[...], values_ref, 0)
    step = min(rows, ROWS)
    attend(
        q_ref,
        [own_ref],
        values_ref,
        [(row, step, 0, rows) for row in range(0, rows, step)],
        all_seen,
        None,
        keep_state(sums_ref, tops_ref),
    )


def more_butterfly_kernel(levels, last, *refs):
    blocks, refs = refs[: len(levels)], refs[len(levels) :]
    (shown_ref, own_ref, q_ref, sums_ref, tops_ref), refs = refs[:5], refs[5:]
    rows = q_ref.shape[1]
    if last:
        hidden_ref, out_w_ref, out_ref, values_ref, keys_ref, all_sums_ref = refs
        sink = keep_sums(all_sums_ref)
    else:
        sums_out_ref, tops_out_ref, values_ref, keys_ref = refs
        sink = keep_state(sums_out_ref, tops_out_ref)
    key_width = own_ref.shape[1] // 2
    for n, (level, block) in enumerate(zip(levels, blocks)):
        spot = pl.ds(n * rows, rows)
        shown = shown_ref[level, :1, :]
        for c in range(0, key_width, LANES):
            keys = block[:, c : c + LANES]
            here = jnp.broadcast_to(shown, keys.shape) > 0
            keys_ref[spot, c : c + LANES] = jnp.where(here, keys, own_ref[:, c : c + LANES])
        spread_values(block[...], values_ref, n * rows, shown)
    step = min(rows, ROWS)
    attend(
        q_ref,
        [keys_ref],
        values_ref,
        [(row, step, 0, rows * len(levels)) for row in range(0, rows, step)],
        all_seen,
        (sums_ref, tops_ref),
        sink,
    )
    if last:
        out_ref[...] = (
            dot(divide_pairs(all_sums_ref), out_w_ref[...]) + hidden_ref[...].astype(jnp.float32)
        ).astype(jnp.bfloat16)


def exchange_edges(block, parity):
    groups, count = lax.axis_size("groups"), lax.axis_size("seq")
    rows = block.shape[0]
    if rows > WIN:
        first = jnp.where(lax.rem(lax.axis_index("seq"), 2) == parity, rows - WIN, 0)
        block = lax.dynamic_slice_in_dim(block, first, WIN, 0)
    route = []
    for group in range(groups):
        for i in range(count):
            other, to = group, i + 1 if i % 2 == parity else i - 1
            if not 0 <= to < count:
                other, to = (group ^ 1 if group ^ 1 < groups else group), i
            route.append((group * count + i, other * count + to))
    return lax.ppermute(block, ("groups", "seq"), route)


def shards(
    residual,
    layer_queries,
    layer_keyvals,
    head_window_extent,
    block_mask,
    first_out,
    second_query,
    second_keyval,
    second_out,
):
    rows, width = residual.shape
    q_width = layer_queries.shape[1]
    kv_width = layer_keyvals.shape[1]
    kv_heads = kv_width // (2 * HEAD_SIZE)
    heads = q_width // HEAD_SIZE
    count = lax.axis_size("seq")
    level_count = count.bit_length() - 1
    bf16, f32 = jnp.bfloat16, jnp.float32
    vmem = pl.BlockSpec(memory_space=pltpu.VMEM)
    state = [jax.ShapeDtypeStruct((heads, rows, LANES), f32)] * 2
    queries = jax.ShapeDtypeStruct((heads, rows, LANES), bf16)
    wide = jax.ShapeDtypeStruct((rows, width), bf16)
    all_sums = pltpu.VMEM((heads, rows, LANES), f32)

    def call(kernel, name, in_specs, out_shape, scratch, key_rows, extra_macs, args):
        macs = 4 * rows * heads * HEAD_SIZE * key_rows + extra_macs
        values = pltpu.VMEM((kv_heads, 2, key_rows, LANES), bf16)
        return pl.pallas_call(
            kernel,
            out_shape=out_shape,
            in_specs=in_specs,
            out_specs=jax.tree.map(lambda _: vmem, out_shape),
            scratch_shapes=[values] + scratch,
            compiler_params=pltpu.CompilerParams(vmem_limit_bytes=VMEM_LIMIT),
            cost_estimate=pl.CostEstimate(
                flops=16 * macs, bytes_accessed=2**21, transcendentals=rows * heads * key_rows
            ),
            name=name,
        )(*args)

    even, odd = (exchange_edges(layer_keyvals, parity) for parity in range(2))
    extents, q_here, sums, tops = call(
        own_window_kernel,
        "own_window",
        [vmem] * 3,
        [jax.ShapeDtypeStruct((heads, 8, LANES), jnp.int32), queries] + state,
        [],
        rows,
        0,
        (head_window_extent.reshape(1, heads), layer_queries, layer_keyvals),
    )
    hidden, normed, keyvals = call(
        halo_window_kernel,
        "halo_window",
        [vmem] * 9,
        [wide, wide, jax.ShapeDtypeStruct((rows, kv_width), bf16)],
        [pltpu.VMEM((2 * WIN, kv_width // 2), bf16), all_sums],
        2 * WIN,
        rows * width * (q_width + kv_width),
        (
            extents,
            q_here,
            even,
            odd,
            sums,
            tops,
            residual,
            first_out,
            second_keyval,
        ),
    )

    others = [None] * level_count
    for level in reversed(range(level_count)):
        route = [(i, i ^ (1 << level)) for i in range(count)]
        others[level] = lax.ppermute(keyvals, "seq", route)
    queries_two, sums, tops, shown = call(
        functools.partial(own_butterfly_kernel, level_count),
        "own_butterfly",
        [vmem] * 4,
        [queries] + state + [jax.ShapeDtypeStruct((level_count, 16, LANES), bf16)],
        [],
        rows,
        rows * width * q_width,
        (block_mask, normed, second_query, keyvals),
    )
    far = level_count - 1
    groups = [list(reversed(range(far))), [far]]


    def key_block(levels):
        return pltpu.VMEM((rows * len(levels), kv_width // 2), bf16)

    for levels in groups[:-1]:
        sums, tops = call(
            functools.partial(more_butterfly_kernel, levels, False),
            "near_butterfly",
            [vmem] * (5 + len(levels)),
            state,
            [key_block(levels)],
            rows * len(levels),
            0,
            (*[others[level] for level in levels], shown, keyvals, queries_two, sums, tops),
        )
    levels = groups[-1]
    return call(
        functools.partial(more_butterfly_kernel, levels, True),
        "far_butterfly",
        [vmem] * (7 + len(levels)),
        wide,
        [key_block(levels), all_sums],
        rows * len(levels),
        rows * width * q_width,
        (*[others[level] for level in levels], shown, keyvals, queries_two, sums, tops, hidden, second_out),
    )


def solution(mesh):
    tokens = P(("groups", "seq"), None)
    placed = (tokens, tokens, tokens, P(), P("seq", None), P(), P(), P(), P())
    return jax.shard_map(shards, mesh=mesh, in_specs=placed, out_specs=tokens, check_vma=False)
```

```python
import functools
import math

import jax
import jax.numpy as jnp
from jax import lax
from jax.experimental import pallas as pl
from jax.experimental.pallas import tpu as pltpu
from jax.sharding import PartitionSpec as P

HEAD_SIZE = 64
WIN = 256
LANES = 128
LOW = -1e30
SCALE = HEAD_SIZE**-0.5 * math.log2(math.e)
VMEM_LIMIT = 20 * 2**20
ROWS = 256


def dot(a, b):
    return jnp.dot(a, b, preferred_element_type=jnp.float32)


def dot_t(a, b):
    return lax.dot_general(a, b, (((1,), (1,)), ((), ())), preferred_element_type=jnp.float32)


def swap_halves(tile):
    return jnp.concatenate([tile[:, HEAD_SIZE:], tile[:, :HEAD_SIZE]], axis=1)


def low_half(rows):
    return lax.broadcasted_iota(jnp.int32, (rows, LANES), 1) < HEAD_SIZE


def splat(row, index, shape):
    lane = lax.broadcasted_iota(jnp.int32, row.shape, 1)
    one = jnp.sum(jnp.where(lane == index, row.astype(jnp.float32), 0.0), axis=1, keepdims=True)
    return jnp.broadcast_to(one, shape)


def spread_queries(queries, kv_heads, spread_ref):
    rows, width = queries.shape
    heads = width // HEAD_SIZE
    low = low_half(rows)
    for head in range(heads):
        at, want = head % 2, head * kv_heads // heads % 2
        tile = queries[:, head // 2 * LANES : (head // 2 + 1) * LANES]
        if at != want:
            tile = swap_halves(tile)
        here = low if want == 0 else jnp.logical_not(low)
        spread_ref[head] = jnp.where(here, tile, jnp.zeros_like(tile))


def spread_values(keyvals, values_ref, first, shown=None):
    rows, width = keyvals.shape
    kv_heads = width // (2 * HEAD_SIZE)
    low = low_half(rows)
    for g in range(kv_heads):
        begin = width // 2 + g // 2 * LANES
        tile = keyvals[:, begin : begin + LANES]
        other = swap_halves(tile)
        for s in range(2):
            here = low if s == 0 else jnp.logical_not(low)
            out = jnp.where(here, tile if g % 2 == s else other, jnp.ones_like(tile))
            if shown is not None:
                out = out * shown
            values_ref[g, s, pl.ds(first, rows), :] = out


def attend(q_ref, key_refs, values_ref, parts, mask, prior, sink):
    heads = q_ref.shape[0]
    kv_heads = values_ref.shape[0]
    steps = [
        (g, s, [h for h in range(heads) if h * kv_heads // heads == g and h % 2 == s], part)
        for g in range(kv_heads)
        for s in range(2)
        for part in range(len(parts))
    ]

    def score(g, s, mine, part):
        row, rows, key, span = parts[part]
        q = jnp.concatenate([q_ref[h, pl.ds(row, rows), :] for h in mine], axis=0)
        tiles, at = [], 0
        for ref in key_refs:
            begin, end = max(key - at, 0), min(key + span - at, ref.shape[0])
            if begin < end:
                keys = ref[pl.ds(begin, end - begin), pl.ds(g // 2 * LANES, LANES)]
                scores = dot_t(q, keys)
                tiles += [scores[:, c : c + LANES] for c in range(0, end - begin, LANES)]
            at += ref.shape[0]
        return tiles

    def mix(g, s, mine, part, tiles):
        row, rows, key, span = parts[part]
        here = pl.ds(row, rows)
        weights, tops, scales = [], [], []
        for n, h in enumerate(mine):
            some = mask(h, part, [tile[n * rows : (n + 1) * rows] for tile in tiles])
            top = jnp.max(functools.reduce(jnp.maximum, some), axis=1, keepdims=True)
            top = jnp.broadcast_to(top, (rows, LANES))
            if prior is not None:
                old = prior[1][h, here, :]
                top = jnp.maximum(top, old)
                scales.append(jnp.exp2((old - top) * SCALE))
            tops.append(top)
            weights.append(
                jnp.concatenate(
                    [jnp.exp2((tile - top) * SCALE).astype(jnp.bfloat16) for tile in some], axis=1
                )
            )
        sums = dot(jnp.concatenate(weights, axis=0), values_ref[g, s, pl.ds(key, span), :])
        for n, h in enumerate(mine):
            one = sums[n * rows : (n + 1) * rows]
            if prior is not None:
                one = one + prior[0][h, here, :] * scales[n]
            sink(h, here, one, tops[n])

    tiles = score(*steps[0])
    for n, step in enumerate(steps):
        ahead = score(*steps[n + 1]) if n + 1 < len(steps) else None
        mix(*step, tiles)
        tiles = ahead


def keep_state(sums_ref, tops_ref):
    def sink(head, here, sums, top):
        sums_ref[head, here, :] = sums
        tops_ref[head, here, :] = top

    return sink


def keep_sums(sums_ref):
    def sink(head, here, sums, top):
        sums_ref[head, here, :] = sums

    return sink


def divide_pairs(sums_ref):
    heads, rows, _ = sums_ref.shape
    low = low_half(rows)
    out = []
    for head in range(0, heads, 2):
        even, odd = sums_ref[head], sums_ref[head + 1]
        total = swap_halves(jnp.where(low, odd, even))
        out.append((jnp.where(low, even, odd) / total).astype(jnp.bfloat16))
    return jnp.concatenate(out, axis=1)


def window_mask(extents_ref, places, valid):
    def mask(head, part, tiles):
        extent = extents_ref[head, :1, :]
        shape = tiles[0].shape
        gap = lax.broadcasted_iota(jnp.int32, shape, 0) - lax.broadcasted_iota(jnp.int32, shape, 1)
        out = []
        for tile, (ahead, outer) in zip(tiles, places[part]):
            reach = jnp.where(valid, extent, -1) if outer else extent
            if ahead <= -shape[1]:
                seen = gap <= reach + ahead
            elif ahead >= shape[0]:
                seen = gap >= ahead - reach
            else:
                seen = jnp.abs(gap - ahead) <= reach
            out.append(jnp.where(seen, tile, LOW))
        return out

    return mask


def window_parts(rows, begin, end):
    parts, places = [], []
    for row in range(0, rows, LANES):
        near = [k for k in range(begin, end, LANES) if -WIN - LANES < k - row < WIN + LANES]
        near = near or [begin]
        parts.append((row, LANES, near[0] - begin, len(near) * LANES))
        places.append([(k - row, not 0 <= k < rows) for k in near])
    return parts, places


def on_side(parity, run):
    me, last = lax.axis_index("seq"), lax.axis_size("seq") - 1
    is_right = lax.rem(me, 2) == parity
    pl.when(is_right)(lambda: run(True, me < last))
    pl.when(jnp.logical_not(is_right))(lambda: run(False, me > 0))


def own_window_kernel(
    extent_ref, queries_ref, own_ref, even_ref, extents_ref, q_ref, sums_ref, tops_ref, values_ref
):
    rows = own_ref.shape[0]
    for head in range(extents_ref.shape[0]):
        one = splat(extent_ref[...], head, extents_ref.shape[1:])
        extents_ref[head] = one.astype(jnp.int32)
    spread_queries(queries_ref[...], values_ref.shape[0], q_ref)

    def run(right, valid):
        begin, refs = (0, [own_ref, even_ref]) if right else (-WIN, [even_ref, own_ref])
        at = 0
        for ref in refs:
            spread_values(ref[...], values_ref, at)
            at += ref.shape[0]
        parts, places = window_parts(rows, begin, begin + at)
        attend(
            q_ref,
            refs,
            values_ref,
            parts,
            window_mask(extents_ref, places, valid),
            None,
            keep_state(sums_ref, tops_ref),
        )

    on_side(0, run)


def halo_window_kernel(
    extents_ref,
    q_ref,
    odd_ref,
    sums_ref,
    tops_ref,
    residual_ref,
    out_w_ref,
    kv_w_ref,
    hidden_ref,
    normed_ref,
    kv_ref,
    values_ref,
    all_sums_ref,
):
    rows = q_ref.shape[1]
    spread_values(odd_ref[...], values_ref, 0)

    def run(right, valid):
        begin = rows if right else -WIN
        parts, places = window_parts(rows, begin, begin + WIN)
        attend(
            q_ref,
            [odd_ref],
            values_ref,
            parts,
            window_mask(extents_ref, places, valid),
            (sums_ref, tops_ref),
            keep_sums(all_sums_ref),
        )

    on_side(1, run)
    hidden = (
        dot(divide_pairs(all_sums_ref), out_w_ref[...]) + residual_ref[...].astype(jnp.float32)
    ).astype(jnp.bfloat16)
    hidden_ref[...] = hidden
    values = hidden.astype(jnp.float32)
    scale = lax.rsqrt(jnp.mean(values * values, axis=-1, keepdims=True) + 1e-05)
    normed = (values * scale).astype(jnp.bfloat16)
    normed_ref[...] = normed
    kv_ref[...] = dot(normed, kv_w_ref[...]).astype(jnp.bfloat16)


def all_seen(head, part, tiles):
    return tiles


def place_blocks(levels, blocks, own_ref, shown_ref, keys_ref, values_ref, first):
    rows = own_ref.shape[0]
    for n, (level, block) in enumerate(zip(levels, blocks)):
        shown = shown_ref[level, :1, :]
        for c in range(0, own_ref.shape[1] // 2, LANES):
            keys = block[:, c : c + LANES]
            here = jnp.broadcast_to(shown, keys.shape) > 0
            keys_ref[pl.ds(n * rows, rows), c : c + LANES] = jnp.where(
                here, keys, own_ref[:, c : c + LANES]
            )
        spread_values(block[...], values_ref, first + n * rows, shown)


def own_butterfly_kernel(levels, *refs):
    blocks, refs = refs[: len(levels)], refs[len(levels) :]
    (mask_ref, normed_ref, q_w_ref, own_ref), refs = refs[:4], refs[4:]
    q_ref, sums_ref, tops_ref, shown_ref, values_ref, keys_ref = refs
    rows = normed_ref.shape[0]
    kv_heads = values_ref.shape[0]
    for level in range(shown_ref.shape[0]):
        one = splat(mask_ref[...], level, shown_ref.shape[1:])
        shown_ref[level] = jnp.where(one == 1.0, 1.0, 0.0).astype(jnp.bfloat16)
    spread_queries(
        dot(normed_ref[...], q_w_ref[...]).astype(jnp.bfloat16), kv_heads, q_ref
    )
    spread_values(own_ref[...], values_ref, 0)
    place_blocks(levels, blocks, own_ref, shown_ref, keys_ref, values_ref, rows)
    step = min(rows, ROWS)
    attend(
        q_ref,
        [own_ref, keys_ref],
        values_ref,
        [(row, step, 0, rows * (1 + len(levels))) for row in range(0, rows, step)],
        all_seen,
        None,
        keep_state(sums_ref, tops_ref),
    )


def more_butterfly_kernel(levels, last, *refs):
    blocks, refs = refs[: len(levels)], refs[len(levels) :]
    (shown_ref, own_ref, q_ref, sums_ref, tops_ref), refs = refs[:5], refs[5:]
    rows = q_ref.shape[1]
    if last:
        hidden_ref, out_w_ref, out_ref, values_ref, keys_ref, all_sums_ref = refs
        sink = keep_sums(all_sums_ref)
    else:
        sums_out_ref, tops_out_ref, values_ref, keys_ref = refs
        sink = keep_state(sums_out_ref, tops_out_ref)
    place_blocks(levels, blocks, own_ref, shown_ref, keys_ref, values_ref, 0)
    step = min(rows, ROWS)
    attend(
        q_ref,
        [keys_ref],
        values_ref,
        [(row, step, 0, rows * len(levels)) for row in range(0, rows, step)],
        all_seen,
        (sums_ref, tops_ref),
        sink,
    )
    if last:
        out_ref[...] = (
            dot(divide_pairs(all_sums_ref), out_w_ref[...]) + hidden_ref[...].astype(jnp.float32)
        ).astype(jnp.bfloat16)


def exchange_edges(block, parity):
    groups, count = lax.axis_size("groups"), lax.axis_size("seq")
    rows = block.shape[0]
    if rows > WIN:
        first = jnp.where(lax.rem(lax.axis_index("seq"), 2) == parity, rows - WIN, 0)
        block = lax.dynamic_slice_in_dim(block, first, WIN, 0)
    route = []
    for group in range(groups):
        for i in range(count):
            other, to = group, i + 1 if i % 2 == parity else i - 1
            if not 0 <= to < count:
                other, to = (group ^ 1 if group ^ 1 < groups else group), i
            route.append((group * count + i, other * count + to))
    return lax.ppermute(block, ("groups", "seq"), route)


def shards(
    residual,
    layer_queries,
    layer_keyvals,
    head_window_extent,
    block_mask,
    first_out,
    second_query,
    second_keyval,
    second_out,
):
    rows, width = residual.shape
    q_width = layer_queries.shape[1]
    kv_width = layer_keyvals.shape[1]
    kv_heads = kv_width // (2 * HEAD_SIZE)
    heads = q_width // HEAD_SIZE
    count = lax.axis_size("seq")
    level_count = count.bit_length() - 1
    bf16, f32 = jnp.bfloat16, jnp.float32
    vmem = pl.BlockSpec(memory_space=pltpu.VMEM)
    state = [jax.ShapeDtypeStruct((heads, rows, LANES), f32)] * 2
    queries = jax.ShapeDtypeStruct((heads, rows, LANES), bf16)
    wide = jax.ShapeDtypeStruct((rows, width), bf16)
    all_sums = pltpu.VMEM((heads, rows, LANES), f32)

    def call(kernel, name, in_specs, out_shape, scratch, key_rows, extra_macs, args):
        macs = 4 * rows * heads * HEAD_SIZE * key_rows + extra_macs
        values = pltpu.VMEM((kv_heads, 2, key_rows, LANES), bf16)
        return pl.pallas_call(
            kernel,
            out_shape=out_shape,
            in_specs=in_specs,
            out_specs=jax.tree.map(lambda _: vmem, out_shape),
            scratch_shapes=[values] + scratch,
            compiler_params=pltpu.CompilerParams(vmem_limit_bytes=VMEM_LIMIT),
            cost_estimate=pl.CostEstimate(
                flops=16 * macs, bytes_accessed=2**21, transcendentals=rows * heads * key_rows
            ),
            name=name,
        )(*args)

    even, odd = (exchange_edges(layer_keyvals, parity) for parity in range(2))
    extents, q_here, sums, tops = call(
        own_window_kernel,
        "own_window",
        [vmem] * 4,
        [jax.ShapeDtypeStruct((heads, 8, LANES), jnp.int32), queries] + state,
        [],
        rows + WIN,
        0,
        (head_window_extent.reshape(1, heads), layer_queries, layer_keyvals, even),
    )
    hidden, normed, keyvals = call(
        halo_window_kernel,
        "halo_window",
        [vmem] * 8,
        [wide, wide, jax.ShapeDtypeStruct((rows, kv_width), bf16)],
        [all_sums],
        WIN,
        rows * width * (q_width + kv_width),
        (
            extents,
            q_here,
            odd,
            sums,
            tops,
            residual,
            first_out,
            second_keyval,
        ),
    )

    others = [None] * level_count
    for level in reversed(range(level_count)):
        route = [(i, i ^ (1 << level)) for i in range(count)]
        others[level] = lax.ppermute(keyvals, "seq", route)
    groups = [[0], [], list(reversed(range(1, level_count)))]
    first, groups = groups[0], [levels for levels in groups[1:] if levels]

    def key_block(levels):
        return pltpu.VMEM((rows * max(len(levels), 1), kv_width // 2), bf16)

    queries_two, sums, tops, shown = call(
        functools.partial(own_butterfly_kernel, first),
        "own_butterfly",
        [vmem] * (4 + len(first)),
        [queries] + state + [jax.ShapeDtypeStruct((level_count, 16, LANES), bf16)],
        [key_block(first)],
        rows * (1 + len(first)),
        rows * width * q_width,
        (*[others[level] for level in first], block_mask, normed, second_query, keyvals),
    )
    for levels in groups[:-1]:
        sums, tops = call(
            functools.partial(more_butterfly_kernel, levels, False),
            "near_butterfly",
            [vmem] * (5 + len(levels)),
            state,
            [key_block(levels)],
            rows * len(levels),
            0,
            (*[others[level] for level in levels], shown, keyvals, queries_two, sums, tops),
        )
    levels = groups[-1]
    return call(
        functools.partial(more_butterfly_kernel, levels, True),
        "far_butterfly",
        [vmem] * (7 + len(levels)),
        wide,
        [key_block(levels), all_sums],
        rows * len(levels),
        rows * width * q_width,
        (*[others[level] for level in levels], shown, keyvals, queries_two, sums, tops, hidden, second_out),
    )


def solution(mesh):
    tokens = P(("groups", "seq"), None)
    placed = (tokens, tokens, tokens, P(), P("seq", None), P(), P(), P(), P())
    return jax.shard_map(shards, mesh=mesh, in_specs=placed, out_specs=tokens, check_vma=False)
```

```python
import functools
import math

import jax
import jax.numpy as jnp
from jax import lax
from jax.experimental import pallas as pl
from jax.experimental.pallas import tpu as pltpu
from jax.sharding import PartitionSpec as P

HEAD_SIZE = 64
WIN = 256
LANES = 128
LOW = -1e30
SCALE = HEAD_SIZE**-0.5 * math.log2(math.e)
VMEM_LIMIT = 20 * 2**20
ROWS = 256
STEP = 512
LAST_STEP = 1024
TOTALS = 16


def dot(a, b):
    return jnp.dot(a, b, preferred_element_type=jnp.float32)


def dot_first(a, b):
    return lax.dot_general(a, b, (((0,), (0,)), ((), ())), preferred_element_type=jnp.float32)


def dot_t(a, b):
    return lax.dot_general(a, b, (((1,), (1,)), ((), ())), preferred_element_type=jnp.float32)


def splat(row, index, shape):
    lane = lax.broadcasted_iota(jnp.int32, row.shape, 1)
    one = jnp.sum(jnp.where(lane == index, row.astype(jnp.float32), 0.0), axis=1, keepdims=True)
    return jnp.broadcast_to(one, shape)


def spread_queries(queries, kv_heads, spread_ref):
    rows, width = queries.shape
    heads = width // HEAD_SIZE
    low = lax.broadcasted_iota(jnp.int32, (rows, LANES), 1) < HEAD_SIZE
    for head in range(heads):
        at, want = head % 2, head * kv_heads // heads % 2
        tile = queries[:, head // 2 * LANES : (head // 2 + 1) * LANES]
        if at != want:
            tile = jnp.concatenate([tile[:, HEAD_SIZE:], tile[:, :HEAD_SIZE]], axis=1)
        here = low if want == 0 else jnp.logical_not(low)
        spread_ref[head] = jnp.where(here, tile, jnp.zeros_like(tile))


def spread_values(keyvals, values_ref, first, shown=None):
    rows, width = keyvals.shape
    kv_heads = values_ref.shape[0]
    for begin in range(0, width // 2, LANES):
        tile = jnp.transpose(keyvals[:, width // 2 + begin : width // 2 + begin + LANES])
        if shown is not None:
            tile = tile * shown
        for g in range(begin // HEAD_SIZE, min((begin + LANES) // HEAD_SIZE, kv_heads)):
            at = g * HEAD_SIZE - begin
            values_ref[g, :HEAD_SIZE, pl.ds(first, rows)] = tile[at : at + HEAD_SIZE]
    one = jnp.ones((TOTALS, rows), jnp.bfloat16)
    for g in range(kv_heads):
        values_ref[g, HEAD_SIZE:, pl.ds(first, rows)] = one if shown is None else one * shown


def attend(q_ref, key_refs, values_ref, parts, mask, prior, sink, columns=STEP):
    heads = q_ref.shape[0]
    kv_heads = values_ref.shape[0]
    group = heads // kv_heads
    steps = []
    for part, (row, rows, key, span) in enumerate(parts):
        many = max(columns // rows, 1)
        for head in range(0, heads, group):
            for h in range(head, head + group, many):
                steps.append((part, list(range(h, min(h + many, head + group)))))

    def score(part, mine):
        row, rows, key, span = parts[part]
        q = jnp.concatenate([q_ref[h, pl.ds(row, rows), :] for h in mine], axis=0)
        lanes = pl.ds(mine[0] // group // 2 * LANES, LANES)
        scores, at = [], 0
        for ref in key_refs:
            begin, end = max(key - at, 0), min(key + span - at, ref.shape[0])
            if begin < end:
                scores.append(dot_t(ref[pl.ds(begin, end - begin), lanes], q))
            at += ref.shape[0]
        return jnp.concatenate(scores, axis=0)

    def mix(part, mine, scores):
        row, rows, key, span = parts[part]
        here = pl.ds(row, rows)
        weights, tops, scales = [], [], []
        for n, h in enumerate(mine):
            some = mask(h, part, scores[:, n * rows : (n + 1) * rows])
            top = jnp.max(some, axis=0, keepdims=True)
            if prior is not None:
                old = prior[1][h, :1, here]
                top = jnp.maximum(top, old)
                scales.append(jnp.exp2((old - top) * SCALE))
            tops.append(top)
            weights.append(jnp.exp2((some - top) * SCALE).astype(jnp.bfloat16))
        sums = dot(
            values_ref[mine[0] // group, :, pl.ds(key, span)], jnp.concatenate(weights, axis=1)
        )
        for n, h in enumerate(mine):
            one = sums[:, n * rows : (n + 1) * rows]
            if prior is not None:
                one = one + prior[0][h, :, here] * scales[n]
            sink(h, here, one, tops[n])

    scores = score(*steps[0])
    for n, step in enumerate(steps):
        ahead = score(*steps[n + 1]) if n + 1 < len(steps) else None
        mix(*step, scores)
        scores = ahead


def keep_state(sums_ref, tops_ref):
    def sink(head, here, sums, top):
        sums_ref[head, :, here] = sums
        tops_ref[head, :, here] = jnp.broadcast_to(top, (tops_ref.shape[1], here.size))

    return sink


def keep_heads(attended_ref):
    def sink(head, here, sums, top):
        attended_ref[head * HEAD_SIZE : (head + 1) * HEAD_SIZE, here] = (
            sums[:HEAD_SIZE] / sums[HEAD_SIZE : HEAD_SIZE + 1]
        ).astype(jnp.bfloat16)

    return sink


def window_mask(extents_ref, places, valid):
    def mask(head, part, scores):
        extent = extents_ref[head, :1, :]
        shape = (LANES, scores.shape[1])
        gap = lax.broadcasted_iota(jnp.int32, shape, 1) - lax.broadcasted_iota(jnp.int32, shape, 0)
        out = []
        for n, (ahead, outer) in enumerate(places[part]):
            reach = jnp.where(valid, extent, -1) if outer else extent
            if ahead <= -LANES:
                seen = gap <= reach + ahead
            elif ahead >= LANES:
                seen = gap >= ahead - reach
            else:
                seen = jnp.abs(gap - ahead) <= reach
            out.append(jnp.where(seen, scores[n * LANES : (n + 1) * LANES], LOW))
        return jnp.concatenate(out, axis=0)

    return mask


def window_parts(rows, begin, end):
    parts, places = [], []
    for row in range(0, rows, LANES):
        near = [k for k in range(begin, end, LANES) if -WIN - LANES < k - row < WIN + LANES]
        near = near or [begin]
        parts.append((row, LANES, near[0] - begin, len(near) * LANES))
        places.append([(k - row, not 0 <= k < rows) for k in near])
    return parts, places


def on_side(parity, run):
    me, last = lax.axis_index("seq"), lax.axis_size("seq") - 1
    is_right = lax.rem(me, 2) == parity
    pl.when(is_right)(lambda: run(True, me < last))
    pl.when(jnp.logical_not(is_right))(lambda: run(False, me > 0))


def own_window_kernel(
    extent_ref, queries_ref, own_ref, even_ref, extents_ref, q_ref, sums_ref, tops_ref, values_ref
):
    rows = own_ref.shape[0]
    for head in range(extents_ref.shape[0]):
        one = splat(extent_ref[...], head, extents_ref.shape[1:])
        extents_ref[head] = one.astype(jnp.int32)
    spread_queries(queries_ref[...], values_ref.shape[0], q_ref)

    def run(right, valid):
        begin, refs = (0, [own_ref, even_ref]) if right else (-WIN, [even_ref, own_ref])
        at = 0
        for ref in refs:
            spread_values(ref[...], values_ref, at)
            at += ref.shape[0]
        parts, places = window_parts(rows, begin, begin + at)
        attend(
            q_ref,
            refs,
            values_ref,
            parts,
            window_mask(extents_ref, places, valid),
            None,
            keep_state(sums_ref, tops_ref),
        )

    on_side(0, run)


def halo_window_kernel(
    extents_ref,
    q_ref,
    odd_ref,
    sums_ref,
    tops_ref,
    residual_ref,
    out_w_ref,
    kv_w_ref,
    hidden_ref,
    normed_ref,
    kv_ref,
    values_ref,
    attended_ref,
):
    rows = q_ref.shape[1]
    spread_values(odd_ref[...], values_ref, 0)

    def run(right, valid):
        begin = rows if right else -WIN
        parts, places = window_parts(rows, begin, begin + WIN)
        attend(
            q_ref,
            [odd_ref],
            values_ref,
            parts,
            window_mask(extents_ref, places, valid),
            (sums_ref, tops_ref),
            keep_heads(attended_ref),
        )

    on_side(1, run)
    hidden = (
        dot_first(attended_ref[...], out_w_ref[...]) + residual_ref[...].astype(jnp.float32)
    ).astype(jnp.bfloat16)
    hidden_ref[...] = hidden
    values = hidden.astype(jnp.float32)
    scale = lax.rsqrt(jnp.mean(values * values, axis=-1, keepdims=True) + 1e-05)
    normed = (values * scale).astype(jnp.bfloat16)
    normed_ref[...] = normed
    kv_ref[...] = dot(normed, kv_w_ref[...]).astype(jnp.bfloat16)


def all_seen(head, part, scores):
    return scores


def place_blocks(levels, blocks, own_ref, shown_ref, keys_ref, values_ref, first):
    rows = own_ref.shape[0]
    for n, (level, block) in enumerate(zip(levels, blocks)):
        shown = shown_ref[level, :1, :]
        wide = jnp.concatenate([shown] * (rows // LANES), axis=1)
        for c in range(0, own_ref.shape[1] // 2, LANES):
            keys = block[:, c : c + LANES]
            here = jnp.broadcast_to(shown, keys.shape) > 0
            keys_ref[pl.ds(n * rows, rows), c : c + LANES] = jnp.where(
                here, keys, own_ref[:, c : c + LANES]
            )
        spread_values(block[...], values_ref, first + n * rows, wide)


def own_butterfly_kernel(levels, *refs):
    blocks, refs = refs[: len(levels)], refs[len(levels) :]
    (mask_ref, normed_ref, q_w_ref, own_ref), refs = refs[:4], refs[4:]
    q_ref, sums_ref, tops_ref, shown_ref, values_ref, keys_ref = refs
    rows = normed_ref.shape[0]
    kv_heads = values_ref.shape[0]
    for level in range(shown_ref.shape[0]):
        one = splat(mask_ref[...], level, shown_ref.shape[1:])
        shown_ref[level] = jnp.where(one == 1.0, 1.0, 0.0).astype(jnp.bfloat16)
    spread_queries(
        dot(normed_ref[...], q_w_ref[...]).astype(jnp.bfloat16), kv_heads, q_ref
    )
    spread_values(own_ref[...], values_ref, 0)
    place_blocks(levels, blocks, own_ref, shown_ref, keys_ref, values_ref, rows)
    step = min(rows, ROWS)
    attend(
        q_ref,
        [own_ref, keys_ref],
        values_ref,
        [(row, step, 0, rows * (1 + len(levels))) for row in range(0, rows, step)],
        all_seen,
        None,
        keep_state(sums_ref, tops_ref),
    )


def more_butterfly_kernel(levels, last, *refs):
    blocks, refs = refs[: len(levels)], refs[len(levels) :]
    (shown_ref, own_ref, q_ref, sums_ref, tops_ref), refs = refs[:5], refs[5:]
    rows = q_ref.shape[1]
    if last:
        hidden_ref, out_w_ref, out_ref, values_ref, keys_ref, attended_ref = refs
        sink = keep_heads(attended_ref)
    else:
        sums_out_ref, tops_out_ref, values_ref, keys_ref = refs
        sink = keep_state(sums_out_ref, tops_out_ref)
    place_blocks(levels, blocks, own_ref, shown_ref, keys_ref, values_ref, 0)
    step = min(rows, ROWS)
    attend(
        q_ref,
        [keys_ref],
        values_ref,
        [(row, step, 0, rows * len(levels)) for row in range(0, rows, step)],
        all_seen,
        (sums_ref, tops_ref),
        sink,
        LAST_STEP,
    )
    if last:
        out_ref[...] = (
            dot_first(attended_ref[...], out_w_ref[...]) + hidden_ref[...].astype(jnp.float32)
        ).astype(jnp.bfloat16)


def exchange_edges(block, parity):
    groups, count = lax.axis_size("groups"), lax.axis_size("seq")
    rows = block.shape[0]
    if rows > WIN:
        first = jnp.where(lax.rem(lax.axis_index("seq"), 2) == parity, rows - WIN, 0)
        block = lax.dynamic_slice_in_dim(block, first, WIN, 0)
    route = []
    for group in range(groups):
        for i in range(count):
            other, to = group, i + 1 if i % 2 == parity else i - 1
            if not 0 <= to < count:
                other, to = (group ^ 1 if group ^ 1 < groups else group), i
            route.append((group * count + i, other * count + to))
    return lax.ppermute(block, ("groups", "seq"), route)


def shards(
    residual,
    layer_queries,
    layer_keyvals,
    head_window_extent,
    block_mask,
    first_out,
    second_query,
    second_keyval,
    second_out,
):
    rows, width = residual.shape
    q_width = layer_queries.shape[1]
    kv_width = layer_keyvals.shape[1]
    kv_heads = kv_width // (2 * HEAD_SIZE)
    heads = q_width // HEAD_SIZE
    count = lax.axis_size("seq")
    level_count = count.bit_length() - 1
    bf16, f32 = jnp.bfloat16, jnp.float32
    vmem = pl.BlockSpec(memory_space=pltpu.VMEM)
    state = [
        jax.ShapeDtypeStruct((heads, HEAD_SIZE + TOTALS, rows), f32),
        jax.ShapeDtypeStruct((heads, 8, rows), f32),
    ]
    queries = jax.ShapeDtypeStruct((heads, rows, LANES), bf16)
    wide = jax.ShapeDtypeStruct((rows, width), bf16)
    attended = pltpu.VMEM((q_width, rows), bf16)

    def call(kernel, name, in_specs, out_shape, scratch, key_rows, extra_macs, args):
        macs = 4 * rows * heads * HEAD_SIZE * key_rows + extra_macs
        values = pltpu.VMEM((kv_heads, HEAD_SIZE + TOTALS, key_rows), bf16)
        return pl.pallas_call(
            kernel,
            out_shape=out_shape,
            in_specs=in_specs,
            out_specs=jax.tree.map(lambda _: vmem, out_shape),
            scratch_shapes=[values] + scratch,
            compiler_params=pltpu.CompilerParams(vmem_limit_bytes=VMEM_LIMIT),
            cost_estimate=pl.CostEstimate(
                flops=16 * macs, bytes_accessed=2**21, transcendentals=rows * heads * key_rows
            ),
            name=name,
        )(*args)

    even, odd = (exchange_edges(layer_keyvals, parity) for parity in range(2))
    extents, q_here, sums, tops = call(
        own_window_kernel,
        "own_window",
        [vmem] * 4,
        [jax.ShapeDtypeStruct((heads, 8, LANES), jnp.int32), queries] + state,
        [],
        rows + WIN,
        0,
        (head_window_extent.reshape(1, heads), layer_queries, layer_keyvals, even),
    )
    hidden, normed, keyvals = call(
        halo_window_kernel,
        "halo_window",
        [vmem] * 8,
        [wide, wide, jax.ShapeDtypeStruct((rows, kv_width), bf16)],
        [attended],
        WIN,
        rows * width * (q_width + kv_width),
        (
            extents,
            q_here,
            odd,
            sums,
            tops,
            residual,
            first_out,
            second_keyval,
        ),
    )

    others = [None] * level_count
    for level in reversed(range(level_count)):
        route = [(i, i ^ (1 << level)) for i in range(count)]
        others[level] = lax.ppermute(keyvals, "seq", route)
    groups = [[0], [], list(reversed(range(1, level_count)))]
    first, groups = groups[0], [levels for levels in groups[1:] if levels]

    def key_block(levels):
        return pltpu.VMEM((rows * max(len(levels), 1), kv_width // 2), bf16)

    queries_two, sums, tops, shown = call(
        functools.partial(own_butterfly_kernel, first),
        "own_butterfly",
        [vmem] * (4 + len(first)),
        [queries] + state + [jax.ShapeDtypeStruct((level_count, 16, LANES), bf16)],
        [key_block(first)],
        rows * (1 + len(first)),
        rows * width * q_width,
        (*[others[level] for level in first], block_mask, normed, second_query, keyvals),
    )
    for levels in groups[:-1]:
        sums, tops = call(
            functools.partial(more_butterfly_kernel, levels, False),
            "near_butterfly",
            [vmem] * (5 + len(levels)),
            state,
            [key_block(levels)],
            rows * len(levels),
            0,
            (*[others[level] for level in levels], shown, keyvals, queries_two, sums, tops),
        )
    levels = groups[-1]
    return call(
        functools.partial(more_butterfly_kernel, levels, True),
        "far_butterfly",
        [vmem] * (7 + len(levels)),
        wide,
        [key_block(levels), attended],
        rows * len(levels),
        rows * width * q_width,
        (*[others[level] for level in levels], shown, keyvals, queries_two, sums, tops, hidden, second_out),
    )


def solution(mesh):
    tokens = P(("groups", "seq"), None)
    placed = (tokens, tokens, tokens, P(), P("seq", None), P(), P(), P(), P())
    return jax.shard_map(shards, mesh=mesh, in_specs=placed, out_specs=tokens, check_vma=False)
```

```python
import functools
import math

import jax
import jax.numpy as jnp
from jax import lax
from jax.experimental import pallas as pl
from jax.experimental.pallas import tpu as pltpu
from jax.sharding import PartitionSpec as P

HEAD_SIZE = 64
WIN = 256
LANES = 128
LOW = -1e30
SCALE = HEAD_SIZE**-0.5 * math.log2(math.e)
VMEM_LIMIT = 20 * 2**20
ROWS = 256
STEP = 512
LAST_STEP = 1024
TOTALS = 16
PIECE = 128


def dot(a, b):
    return jnp.dot(a, b, preferred_element_type=jnp.float32)


def dot_first(a, b):
    return lax.dot_general(a, b, (((0,), (0,)), ((), ())), preferred_element_type=jnp.float32)


def dot_t(a, b):
    return lax.dot_general(a, b, (((1,), (1,)), ((), ())), preferred_element_type=jnp.float32)


def splat(row, index, shape):
    lane = lax.broadcasted_iota(jnp.int32, row.shape, 1)
    one = jnp.sum(jnp.where(lane == index, row.astype(jnp.float32), 0.0), axis=1, keepdims=True)
    return jnp.broadcast_to(one, shape)


def spread_queries(queries, kv_heads, spread_ref):
    rows, width = queries.shape
    heads = width // HEAD_SIZE
    low = lax.broadcasted_iota(jnp.int32, (rows, LANES), 1) < HEAD_SIZE
    for head in range(heads):
        at, want = head % 2, head * kv_heads // heads % 2
        tile = queries[:, head // 2 * LANES : (head // 2 + 1) * LANES]
        if at != want:
            tile = jnp.concatenate([tile[:, HEAD_SIZE:], tile[:, :HEAD_SIZE]], axis=1)
        here = low if want == 0 else jnp.logical_not(low)
        spread_ref[head] = jnp.where(here, tile, jnp.zeros_like(tile))


def spread_values(keyvals, values_ref, first, shown=None):
    rows, width = keyvals.shape
    kv_heads = values_ref.shape[0]
    for begin in range(0, width // 2, LANES):
        tile = jnp.transpose(keyvals[:, width // 2 + begin : width // 2 + begin + LANES])
        if shown is not None:
            tile = tile * shown
        for g in range(begin // HEAD_SIZE, min((begin + LANES) // HEAD_SIZE, kv_heads)):
            at = g * HEAD_SIZE - begin
            values_ref[g, :HEAD_SIZE, pl.ds(first, rows)] = tile[at : at + HEAD_SIZE]
    one = jnp.ones((TOTALS, rows), jnp.bfloat16)
    for g in range(kv_heads):
        values_ref[g, HEAD_SIZE:, pl.ds(first, rows)] = one if shown is None else one * shown


def attend(q_ref, key_refs, values_ref, parts, mask, prior, sink, columns=STEP):
    heads = q_ref.shape[0]
    kv_heads = values_ref.shape[0]
    group = heads // kv_heads
    steps = []
    for part, (row, rows, key, span) in enumerate(parts):
        many = max(columns // rows, 1)
        for head in range(0, heads, group):
            for h in range(head, head + group, many):
                steps.append((part, list(range(h, min(h + many, head + group)))))

    def score(part, mine):
        row, rows, key, span = parts[part]
        q = jnp.concatenate([q_ref[h, pl.ds(row, rows), :] for h in mine], axis=0)
        lanes = pl.ds(mine[0] // group // 2 * LANES, LANES)
        scores, at = [], 0
        for ref in key_refs:
            begin, end = max(key - at, 0), min(key + span - at, ref.shape[0])
            if begin < end:
                scores.append(dot_t(ref[pl.ds(begin, end - begin), lanes], q))
            at += ref.shape[0]
        return jnp.concatenate(scores, axis=0)

    def mix(part, mine, scores):
        row, rows, key, span = parts[part]
        here = pl.ds(row, rows)
        weights, tops, scales = [], [], []
        for n, h in enumerate(mine):
            some = mask(h, part, scores[:, n * rows : (n + 1) * rows])
            top = jnp.max(some, axis=0, keepdims=True)
            if prior is not None:
                old = prior[1][h, :1, here]
                top = jnp.maximum(top, old)
                scales.append(jnp.exp2((old - top) * SCALE))
            tops.append(top)
            weights.append(jnp.exp2((some - top) * SCALE).astype(jnp.bfloat16))
        sums = dot(
            values_ref[mine[0] // group, :, pl.ds(key, span)], jnp.concatenate(weights, axis=1)
        )
        for n, h in enumerate(mine):
            one = sums[:, n * rows : (n + 1) * rows]
            if prior is not None:
                one = one + prior[0][h, :, here] * scales[n]
            sink(h, here, one, tops[n])

    scores = score(*steps[0])
    for n, step in enumerate(steps):
        ahead = score(*steps[n + 1]) if n + 1 < len(steps) else None
        mix(*step, scores)
        scores = ahead


def keep_state(sums_ref, tops_ref):
    def sink(head, here, sums, top):
        sums_ref[head, :, here] = sums
        tops_ref[head, :, here] = jnp.broadcast_to(top, (tops_ref.shape[1], here.size))

    return sink


def keep_heads(attended_ref):
    def sink(head, here, sums, top):
        attended_ref[head * HEAD_SIZE : (head + 1) * HEAD_SIZE, here] = (
            sums[:HEAD_SIZE] / sums[HEAD_SIZE : HEAD_SIZE + 1]
        ).astype(jnp.bfloat16)

    return sink


def window_mask(extents_ref, places, valid):
    def mask(head, part, scores):
        extent = extents_ref[head, :1, :]
        shape = (LANES, scores.shape[1])
        gap = lax.broadcasted_iota(jnp.int32, shape, 1) - lax.broadcasted_iota(jnp.int32, shape, 0)
        out = []
        for n, (ahead, outer) in enumerate(places[part]):
            reach = jnp.where(valid, extent, -1) if outer else extent
            if ahead <= -LANES:
                seen = gap <= reach + ahead
            elif ahead >= LANES:
                seen = gap >= ahead - reach
            else:
                seen = jnp.abs(gap - ahead) <= reach
            out.append(jnp.where(seen, scores[n * LANES : (n + 1) * LANES], LOW))
        return jnp.concatenate(out, axis=0)

    return mask


def window_parts(rows, begin, end):
    parts, places = [], []
    for row in range(0, rows, LANES):
        near = [k for k in range(begin, end, LANES) if -WIN - LANES < k - row < WIN + LANES]
        near = near or [begin]
        parts.append((row, LANES, near[0] - begin, len(near) * LANES))
        places.append([(k - row, not 0 <= k < rows) for k in near])
    return parts, places


def on_side(parity, run):
    me, last = lax.axis_index("seq"), lax.axis_size("seq") - 1
    is_right = lax.rem(me, 2) == parity
    pl.when(is_right)(lambda: run(True, me < last))
    pl.when(jnp.logical_not(is_right))(lambda: run(False, me > 0))


def own_window_kernel(
    extent_ref, queries_ref, own_ref, even_ref, extents_ref, q_ref, sums_ref, tops_ref, values_ref
):
    rows = own_ref.shape[0]
    for head in range(extents_ref.shape[0]):
        one = splat(extent_ref[...], head, extents_ref.shape[1:])
        extents_ref[head] = one.astype(jnp.int32)
    spread_queries(queries_ref[...], values_ref.shape[0], q_ref)

    def run(right, valid):
        begin, refs = (0, [own_ref, even_ref]) if right else (-WIN, [even_ref, own_ref])
        at = 0
        for ref in refs:
            spread_values(ref[...], values_ref, at)
            at += ref.shape[0]
        parts, places = window_parts(rows, begin, begin + at)
        attend(
            q_ref,
            refs,
            values_ref,
            parts,
            window_mask(extents_ref, places, valid),
            None,
            keep_state(sums_ref, tops_ref),
        )

    on_side(0, run)


def halo_window_kernel(
    extents_ref,
    q_ref,
    odd_ref,
    sums_ref,
    tops_ref,
    residual_ref,
    out_w_ref,
    kv_w_ref,
    hidden_ref,
    normed_ref,
    kv_ref,
    values_ref,
    attended_ref,
):
    rows = q_ref.shape[1]
    spread_values(odd_ref[...], values_ref, 0)

    def run(right, valid):
        begin = rows if right else -WIN
        parts, places = window_parts(rows, begin, begin + WIN)
        attend(
            q_ref,
            [odd_ref],
            values_ref,
            parts,
            window_mask(extents_ref, places, valid),
            (sums_ref, tops_ref),
            keep_heads(attended_ref),
        )

    on_side(1, run)
    def project(here):
        hidden_ref[here, :] = (
            dot_first(attended_ref[:, here], out_w_ref[...])
            + residual_ref[here, :].astype(jnp.float32)
        ).astype(jnp.bfloat16)

    def norm(here):
        values = hidden_ref[here, :].astype(jnp.float32)
        scale = lax.rsqrt(jnp.mean(values * values, axis=-1, keepdims=True) + 1e-05)
        normed = (values * scale).astype(jnp.bfloat16)
        normed_ref[here, :] = normed
        kv_ref[here, :] = dot(normed, kv_w_ref[...]).astype(jnp.bfloat16)

    pieces = [pl.ds(row, PIECE) for row in range(0, rows, PIECE)]
    for n, here in enumerate(pieces):
        project(here)
        if n:
            norm(pieces[n - 1])
    norm(pieces[-1])


def all_seen(head, part, scores):
    return scores


def place_blocks(levels, blocks, own_ref, shown_ref, keys_ref, values_ref, first):
    rows = own_ref.shape[0]
    for n, (level, block) in enumerate(zip(levels, blocks)):
        shown = shown_ref[level, :1, :]
        wide = jnp.concatenate([shown] * (rows // LANES), axis=1)
        for c in range(0, own_ref.shape[1] // 2, LANES):
            keys = block[:, c : c + LANES]
            here = jnp.broadcast_to(shown, keys.shape) > 0
            keys_ref[pl.ds(n * rows, rows), c : c + LANES] = jnp.where(
                here, keys, own_ref[:, c : c + LANES]
            )
        spread_values(block[...], values_ref, first + n * rows, wide)


def own_butterfly_kernel(levels, *refs):
    blocks, refs = refs[: len(levels)], refs[len(levels) :]
    (mask_ref, normed_ref, q_w_ref, own_ref), refs = refs[:4], refs[4:]
    q_ref, sums_ref, tops_ref, shown_ref, values_ref, keys_ref = refs
    rows = normed_ref.shape[0]
    kv_heads = values_ref.shape[0]
    for level in range(shown_ref.shape[0]):
        one = splat(mask_ref[...], level, shown_ref.shape[1:])
        shown_ref[level] = jnp.where(one == 1.0, 1.0, 0.0).astype(jnp.bfloat16)
    spread_queries(
        dot(normed_ref[...], q_w_ref[...]).astype(jnp.bfloat16), kv_heads, q_ref
    )
    spread_values(own_ref[...], values_ref, 0)
    place_blocks(levels, blocks, own_ref, shown_ref, keys_ref, values_ref, rows)
    step = min(rows, ROWS)
    attend(
        q_ref,
        [own_ref, keys_ref],
        values_ref,
        [(row, step, 0, rows * (1 + len(levels))) for row in range(0, rows, step)],
        all_seen,
        None,
        keep_state(sums_ref, tops_ref),
    )


def more_butterfly_kernel(levels, last, *refs):
    blocks, refs = refs[: len(levels)], refs[len(levels) :]
    (shown_ref, own_ref, q_ref, sums_ref, tops_ref), refs = refs[:5], refs[5:]
    rows = q_ref.shape[1]
    if last:
        hidden_ref, out_w_ref, out_ref, values_ref, keys_ref, attended_ref = refs
        sink = keep_heads(attended_ref)
    else:
        sums_out_ref, tops_out_ref, values_ref, keys_ref = refs
        sink = keep_state(sums_out_ref, tops_out_ref)
    place_blocks(levels, blocks, own_ref, shown_ref, keys_ref, values_ref, 0)
    step = min(rows, ROWS)
    attend(
        q_ref,
        [keys_ref],
        values_ref,
        [(row, step, 0, rows * len(levels)) for row in range(0, rows, step)],
        all_seen,
        (sums_ref, tops_ref),
        sink,
        LAST_STEP,
    )
    if last:
        out_ref[...] = (
            dot_first(attended_ref[...], out_w_ref[...]) + hidden_ref[...].astype(jnp.float32)
        ).astype(jnp.bfloat16)


def exchange_edges(block, parity):
    groups, count = lax.axis_size("groups"), lax.axis_size("seq")
    rows = block.shape[0]
    if rows > WIN:
        first = jnp.where(lax.rem(lax.axis_index("seq"), 2) == parity, rows - WIN, 0)
        block = lax.dynamic_slice_in_dim(block, first, WIN, 0)
    route = []
    for group in range(groups):
        for i in range(count):
            other, to = group, i + 1 if i % 2 == parity else i - 1
            if not 0 <= to < count:
                other, to = (group ^ 1 if group ^ 1 < groups else group), i
            route.append((group * count + i, other * count + to))
    return lax.ppermute(block, ("groups", "seq"), route)


def shards(
    residual,
    layer_queries,
    layer_keyvals,
    head_window_extent,
    block_mask,
    first_out,
    second_query,
    second_keyval,
    second_out,
):
    rows, width = residual.shape
    q_width = layer_queries.shape[1]
    kv_width = layer_keyvals.shape[1]
    kv_heads = kv_width // (2 * HEAD_SIZE)
    heads = q_width // HEAD_SIZE
    count = lax.axis_size("seq")
    level_count = count.bit_length() - 1
    bf16, f32 = jnp.bfloat16, jnp.float32
    vmem = pl.BlockSpec(memory_space=pltpu.VMEM)
    state = [
        jax.ShapeDtypeStruct((heads, HEAD_SIZE + TOTALS, rows), f32),
        jax.ShapeDtypeStruct((heads, 8, rows), f32),
    ]
    queries = jax.ShapeDtypeStruct((heads, rows, LANES), bf16)
    wide = jax.ShapeDtypeStruct((rows, width), bf16)
    attended = pltpu.VMEM((q_width, rows), bf16)

    def call(kernel, name, in_specs, out_shape, scratch, key_rows, extra_macs, args):
        macs = 4 * rows * heads * HEAD_SIZE * key_rows + extra_macs
        values = pltpu.VMEM((kv_heads, HEAD_SIZE + TOTALS, key_rows), bf16)
        return pl.pallas_call(
            kernel,
            out_shape=out_shape,
            in_specs=in_specs,
            out_specs=jax.tree.map(lambda _: vmem, out_shape),
            scratch_shapes=[values] + scratch,
            compiler_params=pltpu.CompilerParams(vmem_limit_bytes=VMEM_LIMIT),
            cost_estimate=pl.CostEstimate(
                flops=16 * macs, bytes_accessed=2**21, transcendentals=rows * heads * key_rows
            ),
            name=name,
        )(*args)

    even, odd = (exchange_edges(layer_keyvals, parity) for parity in range(2))
    extents, q_here, sums, tops = call(
        own_window_kernel,
        "own_window",
        [vmem] * 4,
        [jax.ShapeDtypeStruct((heads, 8, LANES), jnp.int32), queries] + state,
        [],
        rows + WIN,
        0,
        (head_window_extent.reshape(1, heads), layer_queries, layer_keyvals, even),
    )
    hidden, normed, keyvals = call(
        halo_window_kernel,
        "halo_window",
        [vmem] * 8,
        [wide, wide, jax.ShapeDtypeStruct((rows, kv_width), bf16)],
        [attended],
        WIN,
        rows * width * (q_width + kv_width),
        (
            extents,
            q_here,
            odd,
            sums,
            tops,
            residual,
            first_out,
            second_keyval,
        ),
    )

    others = [None] * level_count
    for level in reversed(range(level_count)):
        route = [(i, i ^ (1 << level)) for i in range(count)]
        others[level] = lax.ppermute(keyvals, "seq", route)
    groups = [[0], [], list(reversed(range(1, level_count)))]
    first, groups = groups[0], [levels for levels in groups[1:] if levels]

    def key_block(levels):
        return pltpu.VMEM((rows * max(len(levels), 1), kv_width // 2), bf16)

    queries_two, sums, tops, shown = call(
        functools.partial(own_butterfly_kernel, first),
        "own_butterfly",
        [vmem] * (4 + len(first)),
        [queries] + state + [jax.ShapeDtypeStruct((level_count, 16, LANES), bf16)],
        [key_block(first)],
        rows * (1 + len(first)),
        rows * width * q_width,
        (*[others[level] for level in first], block_mask, normed, second_query, keyvals),
    )
    for levels in groups[:-1]:
        sums, tops = call(
            functools.partial(more_butterfly_kernel, levels, False),
            "near_butterfly",
            [vmem] * (5 + len(levels)),
            state,
            [key_block(levels)],
            rows * len(levels),
            0,
            (*[others[level] for level in levels], shown, keyvals, queries_two, sums, tops),
        )
    levels = groups[-1]
    return call(
        functools.partial(more_butterfly_kernel, levels, True),
        "far_butterfly",
        [vmem] * (7 + len(levels)),
        wide,
        [key_block(levels), attended],
        rows * len(levels),
        rows * width * q_width,
        (*[others[level] for level in levels], shown, keyvals, queries_two, sums, tops, hidden, second_out),
    )


def solution(mesh):
    tokens = P(("groups", "seq"), None)
    placed = (tokens, tokens, tokens, P(), P("seq", None), P(), P(), P(), P())
    return jax.shard_map(shards, mesh=mesh, in_specs=placed, out_specs=tokens, check_vma=False)
```

```python
import functools
import math

import jax
import jax.numpy as jnp
from jax import lax
from jax.experimental import pallas as pl
from jax.experimental.pallas import tpu as pltpu
from jax.sharding import PartitionSpec as P

HEAD_SIZE = 64
WIN = 256
LANES = 128
LOW = -1e30
SCALE = HEAD_SIZE**-0.5 * math.log2(math.e)
VMEM_LIMIT = 20 * 2**20
ROWS = 256
STEP = 512
TOTALS = 16
PIECE = 128


def dot(a, b):
    return jnp.dot(a, b, preferred_element_type=jnp.float32)


def dot_first(a, b):
    return lax.dot_general(a, b, (((0,), (0,)), ((), ())), preferred_element_type=jnp.float32)


def dot_t(a, b):
    return lax.dot_general(a, b, (((1,), (1,)), ((), ())), preferred_element_type=jnp.float32)


def splat(row, index, shape):
    lane = lax.broadcasted_iota(jnp.int32, row.shape, 1)
    one = jnp.sum(jnp.where(lane == index, row.astype(jnp.float32), 0.0), axis=1, keepdims=True)
    return jnp.broadcast_to(one, shape)


def spread_queries(queries, kv_heads, spread_ref):
    rows, width = queries.shape
    heads = width // HEAD_SIZE
    low = lax.broadcasted_iota(jnp.int32, (rows, LANES), 1) < HEAD_SIZE
    for head in range(heads):
        at, want = head % 2, head * kv_heads // heads % 2
        tile = queries[:, head // 2 * LANES : (head // 2 + 1) * LANES]
        if at != want:
            tile = jnp.concatenate([tile[:, HEAD_SIZE:], tile[:, :HEAD_SIZE]], axis=1)
        here = low if want == 0 else jnp.logical_not(low)
        spread_ref[head] = jnp.where(here, tile, jnp.zeros_like(tile))


def spread_values(keyvals, values_ref, first, shown=None):
    rows, width = keyvals.shape
    kv_heads = values_ref.shape[0]
    for begin in range(0, width // 2, LANES):
        tile = jnp.transpose(keyvals[:, width // 2 + begin : width // 2 + begin + LANES])
        if shown is not None:
            tile = tile * shown
        for g in range(begin // HEAD_SIZE, min((begin + LANES) // HEAD_SIZE, kv_heads)):
            at = g * HEAD_SIZE - begin
            values_ref[g, :HEAD_SIZE, pl.ds(first, rows)] = tile[at : at + HEAD_SIZE]
    one = jnp.ones((TOTALS, rows), jnp.bfloat16)
    for g in range(kv_heads):
        values_ref[g, HEAD_SIZE:, pl.ds(first, rows)] = one if shown is None else one * shown


def attend(q_ref, key_refs, values_ref, parts, mask, prior, sink):
    heads = q_ref.shape[0]
    kv_heads = values_ref.shape[0]
    group = heads // kv_heads
    steps = []
    for part, (row, rows, key, span) in enumerate(parts):
        many = max(STEP // rows, 1)
        for head in range(0, heads, group):
            for h in range(head, head + group, many):
                steps.append((part, list(range(h, min(h + many, head + group)))))

    def score(part, mine):
        row, rows, key, span = parts[part]
        q = jnp.concatenate([q_ref[h, pl.ds(row, rows), :] for h in mine], axis=0)
        lanes = pl.ds(mine[0] // group // 2 * LANES, LANES)
        scores, at = [], 0
        for ref in key_refs:
            begin, end = max(key - at, 0), min(key + span - at, ref.shape[0])
            if begin < end:
                scores.append(dot_t(ref[pl.ds(begin, end - begin), lanes], q))
            at += ref.shape[0]
        return jnp.concatenate(scores, axis=0)

    def soften(part, mine, scores):
        row, rows, key, span = parts[part]
        here = pl.ds(row, rows)
        weights, tops, scales = [], [], []
        for n, h in enumerate(mine):
            some = mask(h, part, scores[:, n * rows : (n + 1) * rows])
            top = jnp.max(some, axis=0, keepdims=True)
            if prior is not None:
                old = prior[1][h, :1, here]
                top = jnp.maximum(top, old)
                scales.append(jnp.exp2((old - top) * SCALE))
            tops.append(top)
            weights.append(jnp.exp2((some - top) * SCALE).astype(jnp.bfloat16))
        return jnp.concatenate(weights, axis=1), tops, scales

    def mix(part, mine, weights, tops, scales):
        row, rows, key, span = parts[part]
        here = pl.ds(row, rows)
        sums = dot(values_ref[mine[0] // group, :, pl.ds(key, span)], weights)
        for n, h in enumerate(mine):
            one = sums[:, n * rows : (n + 1) * rows]
            if prior is not None:
                one = one + prior[0][h, :, here] * scales[n]
            sink(h, here, one, tops[n])

    scores = [score(*step) for step in steps[:2]]
    for n, step in enumerate(steps):
        if n + 2 < len(steps):
            scores.append(score(*steps[n + 2]))
        mix(*step, *soften(*step, scores[n]))

def keep_state(sums_ref, tops_ref):
    def sink(head, here, sums, top):
        sums_ref[head, :, here] = sums
        tops_ref[head, :, here] = jnp.broadcast_to(top, (tops_ref.shape[1], here.size))

    return sink


def keep_heads(attended_ref):
    def sink(head, here, sums, top):
        attended_ref[head * HEAD_SIZE : (head + 1) * HEAD_SIZE, here] = (
            sums[:HEAD_SIZE] / sums[HEAD_SIZE : HEAD_SIZE + 1]
        ).astype(jnp.bfloat16)

    return sink


def window_mask(extents_ref, places, valid):
    def mask(head, part, scores):
        extent = extents_ref[head, :1, :]
        shape = (LANES, scores.shape[1])
        gap = lax.broadcasted_iota(jnp.int32, shape, 1) - lax.broadcasted_iota(jnp.int32, shape, 0)
        out = []
        for n, (ahead, outer) in enumerate(places[part]):
            reach = jnp.where(valid, extent, -1) if outer else extent
            if ahead <= -LANES:
                seen = gap <= reach + ahead
            elif ahead >= LANES:
                seen = gap >= ahead - reach
            else:
                seen = jnp.abs(gap - ahead) <= reach
            out.append(jnp.where(seen, scores[n * LANES : (n + 1) * LANES], LOW))
        return jnp.concatenate(out, axis=0)

    return mask


def window_parts(rows, begin, end):
    parts, places = [], []
    for row in range(0, rows, LANES):
        near = [k for k in range(begin, end, LANES) if -WIN - LANES < k - row < WIN + LANES]
        near = near or [begin]
        parts.append((row, LANES, near[0] - begin, len(near) * LANES))
        places.append([(k - row, not 0 <= k < rows) for k in near])
    return parts, places


def on_side(parity, run):
    me, last = lax.axis_index("seq"), lax.axis_size("seq") - 1
    is_right = lax.rem(me, 2) == parity
    pl.when(is_right)(lambda: run(True, me < last))
    pl.when(jnp.logical_not(is_right))(lambda: run(False, me > 0))


def own_window_kernel(
    extent_ref, queries_ref, own_ref, even_ref, extents_ref, q_ref, sums_ref, tops_ref, values_ref
):
    rows = own_ref.shape[0]
    for head in range(extents_ref.shape[0]):
        one = splat(extent_ref[...], head, extents_ref.shape[1:])
        extents_ref[head] = one.astype(jnp.int32)
    spread_queries(queries_ref[...], values_ref.shape[0], q_ref)

    def run(right, valid):
        begin, refs = (0, [own_ref, even_ref]) if right else (-WIN, [even_ref, own_ref])
        at = 0
        for ref in refs:
            spread_values(ref[...], values_ref, at)
            at += ref.shape[0]
        parts, places = window_parts(rows, begin, begin + at)
        attend(
            q_ref,
            refs,
            values_ref,
            parts,
            window_mask(extents_ref, places, valid),
            None,
            keep_state(sums_ref, tops_ref),
        )

    on_side(0, run)


def halo_window_kernel(
    extents_ref,
    q_ref,
    odd_ref,
    sums_ref,
    tops_ref,
    residual_ref,
    out_w_ref,
    kv_w_ref,
    hidden_ref,
    normed_ref,
    kv_ref,
    values_ref,
    attended_ref,
):
    rows = q_ref.shape[1]
    spread_values(odd_ref[...], values_ref, 0)

    def run(right, valid):
        begin = rows if right else -WIN
        parts, places = window_parts(rows, begin, begin + WIN)
        attend(
            q_ref,
            [odd_ref],
            values_ref,
            parts,
            window_mask(extents_ref, places, valid),
            (sums_ref, tops_ref),
            keep_heads(attended_ref),
        )

    on_side(1, run)
    def project(here):
        hidden_ref[here, :] = (
            dot_first(attended_ref[:, here], out_w_ref[...])
            + residual_ref[here, :].astype(jnp.float32)
        ).astype(jnp.bfloat16)

    def norm(here):
        values = hidden_ref[here, :].astype(jnp.float32)
        scale = lax.rsqrt(jnp.mean(values * values, axis=-1, keepdims=True) + 1e-05)
        normed = (values * scale).astype(jnp.bfloat16)
        normed_ref[here, :] = normed
        kv_ref[here, :] = dot(normed, kv_w_ref[...]).astype(jnp.bfloat16)

    pieces = [pl.ds(row, PIECE) for row in range(0, rows, PIECE)]
    for n, here in enumerate(pieces):
        project(here)
        if n:
            norm(pieces[n - 1])
    norm(pieces[-1])


def all_seen(head, part, scores):
    return scores


def place_blocks(levels, blocks, own_ref, shown_ref, keys_ref, values_ref, first):
    rows = own_ref.shape[0]
    for n, (level, block) in enumerate(zip(levels, blocks)):
        shown = shown_ref[level, :1, :]
        wide = jnp.concatenate([shown] * (rows // LANES), axis=1)
        for c in range(0, own_ref.shape[1] // 2, LANES):
            keys = block[:, c : c + LANES]
            here = jnp.broadcast_to(shown, keys.shape) > 0
            keys_ref[pl.ds(n * rows, rows), c : c + LANES] = jnp.where(
                here, keys, own_ref[:, c : c + LANES]
            )
        spread_values(block[...], values_ref, first + n * rows, wide)


def own_butterfly_kernel(levels, *refs):
    blocks, refs = refs[: len(levels)], refs[len(levels) :]
    (mask_ref, normed_ref, q_w_ref, own_ref), refs = refs[:4], refs[4:]
    q_ref, sums_ref, tops_ref, shown_ref, values_ref, keys_ref = refs
    rows = normed_ref.shape[0]
    kv_heads = values_ref.shape[0]
    for level in range(shown_ref.shape[0]):
        one = splat(mask_ref[...], level, shown_ref.shape[1:])
        shown_ref[level] = jnp.where(one == 1.0, 1.0, 0.0).astype(jnp.bfloat16)
    spread_queries(
        dot(normed_ref[...], q_w_ref[...]).astype(jnp.bfloat16), kv_heads, q_ref
    )
    spread_values(own_ref[...], values_ref, 0)
    place_blocks(levels, blocks, own_ref, shown_ref, keys_ref, values_ref, rows)
    step = min(rows, ROWS)
    attend(
        q_ref,
        [own_ref, keys_ref],
        values_ref,
        [(row, step, 0, rows * (1 + len(levels))) for row in range(0, rows, step)],
        all_seen,
        None,
        keep_state(sums_ref, tops_ref),
    )


def more_butterfly_kernel(levels, last, *refs):
    blocks, refs = refs[: len(levels)], refs[len(levels) :]
    (shown_ref, own_ref, q_ref, sums_ref, tops_ref), refs = refs[:5], refs[5:]
    rows = q_ref.shape[1]
    if last:
        hidden_ref, out_w_ref, out_ref, values_ref, keys_ref, attended_ref = refs
        sink = keep_heads(attended_ref)
    else:
        sums_out_ref, tops_out_ref, values_ref, keys_ref = refs
        sink = keep_state(sums_out_ref, tops_out_ref)
    place_blocks(levels, blocks, own_ref, shown_ref, keys_ref, values_ref, 0)
    step = min(rows, ROWS)
    attend(
        q_ref,
        [keys_ref],
        values_ref,
        [(row, step, 0, rows * len(levels)) for row in range(0, rows, step)],
        all_seen,
        (sums_ref, tops_ref),
        sink,
    )
    if last:
        out_ref[...] = (
            dot_first(attended_ref[...], out_w_ref[...]) + hidden_ref[...].astype(jnp.float32)
        ).astype(jnp.bfloat16)


def exchange_edges(block, parity):
    groups, count = lax.axis_size("groups"), lax.axis_size("seq")
    rows = block.shape[0]
    if rows > WIN:
        first = jnp.where(lax.rem(lax.axis_index("seq"), 2) == parity, rows - WIN, 0)
        block = lax.dynamic_slice_in_dim(block, first, WIN, 0)
    route = []
    for group in range(groups):
        for i in range(count):
            other, to = group, i + 1 if i % 2 == parity else i - 1
            if not 0 <= to < count:
                other, to = (group ^ 1 if group ^ 1 < groups else group), i
            route.append((group * count + i, other * count + to))
    return lax.ppermute(block, ("groups", "seq"), route)


def shards(
    residual,
    layer_queries,
    layer_keyvals,
    head_window_extent,
    block_mask,
    first_out,
    second_query,
    second_keyval,
    second_out,
):
    rows, width = residual.shape
    q_width = layer_queries.shape[1]
    kv_width = layer_keyvals.shape[1]
    kv_heads = kv_width // (2 * HEAD_SIZE)
    heads = q_width // HEAD_SIZE
    count = lax.axis_size("seq")
    level_count = count.bit_length() - 1
    bf16, f32 = jnp.bfloat16, jnp.float32
    vmem = pl.BlockSpec(memory_space=pltpu.VMEM)
    state = [
        jax.ShapeDtypeStruct((heads, HEAD_SIZE + TOTALS, rows), f32),
        jax.ShapeDtypeStruct((heads, 8, rows), f32),
    ]
    queries = jax.ShapeDtypeStruct((heads, rows, LANES), bf16)
    wide = jax.ShapeDtypeStruct((rows, width), bf16)
    attended = pltpu.VMEM((q_width, rows), bf16)

    def call(kernel, name, in_specs, out_shape, scratch, key_rows, extra_macs, args):
        macs = 4 * rows * heads * HEAD_SIZE * key_rows + extra_macs
        values = pltpu.VMEM((kv_heads, HEAD_SIZE + TOTALS, key_rows), bf16)
        return pl.pallas_call(
            kernel,
            out_shape=out_shape,
            in_specs=in_specs,
            out_specs=jax.tree.map(lambda _: vmem, out_shape),
            scratch_shapes=[values] + scratch,
            compiler_params=pltpu.CompilerParams(vmem_limit_bytes=VMEM_LIMIT),
            cost_estimate=pl.CostEstimate(
                flops=16 * macs, bytes_accessed=2**21, transcendentals=rows * heads * key_rows
            ),
            name=name,
        )(*args)

    even, odd = (exchange_edges(layer_keyvals, parity) for parity in range(2))
    extents, q_here, sums, tops = call(
        own_window_kernel,
        "own_window",
        [vmem] * 4,
        [jax.ShapeDtypeStruct((heads, 8, LANES), jnp.int32), queries] + state,
        [],
        rows + WIN,
        0,
        (head_window_extent.reshape(1, heads), layer_queries, layer_keyvals, even),
    )
    hidden, normed, keyvals = call(
        halo_window_kernel,
        "halo_window",
        [vmem] * 8,
        [wide, wide, jax.ShapeDtypeStruct((rows, kv_width), bf16)],
        [attended],
        WIN,
        rows * width * (q_width + kv_width),
        (
            extents,
            q_here,
            odd,
            sums,
            tops,
            residual,
            first_out,
            second_keyval,
        ),
    )

    others = [None] * level_count
    for level in reversed(range(level_count)):
        route = [(i, i ^ (1 << level)) for i in range(count)]
        others[level] = lax.ppermute(keyvals, "seq", route)
    groups = [[0], [], list(reversed(range(1, level_count)))]
    first, groups = groups[0], [levels for levels in groups[1:] if levels]

    def key_block(levels):
        return pltpu.VMEM((rows * max(len(levels), 1), kv_width // 2), bf16)

    queries_two, sums, tops, shown = call(
        functools.partial(own_butterfly_kernel, first),
        "own_butterfly",
        [vmem] * (4 + len(first)),
        [queries] + state + [jax.ShapeDtypeStruct((level_count, 16, LANES), bf16)],
        [key_block(first)],
        rows * (1 + len(first)),
        rows * width * q_width,
        (*[others[level] for level in first], block_mask, normed, second_query, keyvals),
    )
    for levels in groups[:-1]:
        sums, tops = call(
            functools.partial(more_butterfly_kernel, levels, False),
            "near_butterfly",
            [vmem] * (5 + len(levels)),
            state,
            [key_block(levels)],
            rows * len(levels),
            0,
            (*[others[level] for level in levels], shown, keyvals, queries_two, sums, tops),
        )
    levels = groups[-1]
    return call(
        functools.partial(more_butterfly_kernel, levels, True),
        "far_butterfly",
        [vmem] * (7 + len(levels)),
        wide,
        [key_block(levels), attended],
        rows * len(levels),
        rows * width * q_width,
        (*[others[level] for level in levels], shown, keyvals, queries_two, sums, tops, hidden, second_out),
    )


def solution(mesh):
    tokens = P(("groups", "seq"), None)
    placed = (tokens, tokens, tokens, P(), P("seq", None), P(), P(), P(), P())
    return jax.shard_map(shards, mesh=mesh, in_specs=placed, out_specs=tokens, check_vma=False)
```

```python
import functools
import math

import jax
import jax.numpy as jnp
from jax import lax
from jax.experimental import pallas as pl
from jax.experimental.pallas import tpu as pltpu
from jax.sharding import PartitionSpec as P

HEAD_SIZE = 64
WIN = 256
LANES = 128
LOW = -1e30
SCALE = HEAD_SIZE**-0.5 * math.log2(math.e)
VMEM_LIMIT = 20 * 2**20
ROWS = 256
STEP = 512
TOTALS = 16
PIECE = 128


def dot(a, b):
    return jnp.dot(a, b, preferred_element_type=jnp.float32)


def dot_first(a, b):
    return lax.dot_general(a, b, (((0,), (0,)), ((), ())), preferred_element_type=jnp.float32)


def dot_t(a, b):
    return lax.dot_general(a, b, (((1,), (1,)), ((), ())), preferred_element_type=jnp.float32)


def splat(row, index, shape):
    lane = lax.broadcasted_iota(jnp.int32, row.shape, 1)
    one = jnp.sum(jnp.where(lane == index, row.astype(jnp.float32), 0.0), axis=1, keepdims=True)
    return jnp.broadcast_to(one, shape)


def spread_queries(queries, kv_heads, spread_ref):
    rows, width = queries.shape
    heads = width // HEAD_SIZE
    low = lax.broadcasted_iota(jnp.int32, (rows, LANES), 1) < HEAD_SIZE
    for head in range(heads):
        at, want = head % 2, head * kv_heads // heads % 2
        tile = queries[:, head // 2 * LANES : (head // 2 + 1) * LANES]
        if at != want:
            tile = jnp.concatenate([tile[:, HEAD_SIZE:], tile[:, :HEAD_SIZE]], axis=1)
        here = low if want == 0 else jnp.logical_not(low)
        spread_ref[head] = jnp.where(here, tile, jnp.zeros_like(tile))


def spread_values(keyvals, values_ref, first, shown=None):
    rows, width = keyvals.shape
    kv_heads = values_ref.shape[0]
    for begin in range(0, width // 2, LANES):
        tile = jnp.transpose(keyvals[:, width // 2 + begin : width // 2 + begin + LANES])
        if shown is not None:
            tile = tile * shown
        for g in range(begin // HEAD_SIZE, min((begin + LANES) // HEAD_SIZE, kv_heads)):
            at = g * HEAD_SIZE - begin
            values_ref[g, :HEAD_SIZE, pl.ds(first, rows)] = tile[at : at + HEAD_SIZE]
    one = jnp.ones((TOTALS, rows), jnp.bfloat16)
    for g in range(kv_heads):
        values_ref[g, HEAD_SIZE:, pl.ds(first, rows)] = one if shown is None else one * shown


def attend(q_ref, key_refs, values_ref, parts, mask, prior, sink):
    heads = q_ref.shape[0]
    kv_heads = values_ref.shape[0]
    group = heads // kv_heads
    steps = []
    for part, (row, rows, key, span) in enumerate(parts):
        many = max(STEP // rows, 1)
        for head in range(0, heads, group):
            for h in range(head, head + group, many):
                steps.append((part, list(range(h, min(h + many, head + group)))))

    def score(part, mine):
        row, rows, key, span = parts[part]
        q = jnp.concatenate([q_ref[h, pl.ds(row, rows), :] for h in mine], axis=0)
        lanes = pl.ds(mine[0] // group // 2 * LANES, LANES)
        scores, at = [], 0
        for ref in key_refs:
            begin, end = max(key - at, 0), min(key + span - at, ref.shape[0])
            if begin < end:
                scores.append(dot_t(ref[pl.ds(begin, end - begin), lanes], q))
            at += ref.shape[0]
        return jnp.concatenate(scores, axis=0)

    def soften(part, mine, scores):
        row, rows, key, span = parts[part]
        here = pl.ds(row, rows)
        weights, tops, scales = [], [], []
        for n, h in enumerate(mine):
            some = mask(h, part, scores[:, n * rows : (n + 1) * rows])
            top = jnp.max(some, axis=0, keepdims=True)
            if prior is not None:
                old = prior[1][h, :1, here]
                top = jnp.maximum(top, old)
                scales.append(jnp.exp2((old - top) * SCALE))
            tops.append(top)
            weights.append(jnp.exp2((some - top) * SCALE).astype(jnp.bfloat16))
        return jnp.concatenate(weights, axis=1), tops, scales

    def mix(part, mine, weights, tops, scales):
        row, rows, key, span = parts[part]
        here = pl.ds(row, rows)
        sums = dot(values_ref[mine[0] // group, :, pl.ds(key, span)], weights)
        for n, h in enumerate(mine):
            one = sums[:, n * rows : (n + 1) * rows]
            if prior is not None:
                one = one + prior[0][h, :, here] * scales[n]
            sink(h, here, one, tops[n])

    if len(parts) == 1:
        scores = [score(*step) for step in steps[:2]]
        for n, step in enumerate(steps):
            if n + 2 < len(steps):
                scores.append(score(*steps[n + 2]))
            mix(*step, *soften(*step, scores[n]))
        return
    scores, weights = [score(*step) for step in steps[:2]], []
    for n, step in enumerate(steps):
        weights.append(soften(*step, scores[n]))
        if n + 2 < len(steps):
            scores.append(score(*steps[n + 2]))
        if n:
            mix(*steps[n - 1], *weights[n - 1])
    mix(*steps[-1], *weights[-1])


def keep_state(sums_ref, tops_ref):
    def sink(head, here, sums, top):
        sums_ref[head, :, here] = sums
        tops_ref[head, :, here] = jnp.broadcast_to(top, (tops_ref.shape[1], here.size))

    return sink


def keep_heads(attended_ref):
    def sink(head, here, sums, top):
        attended_ref[head * HEAD_SIZE : (head + 1) * HEAD_SIZE, here] = (
            sums[:HEAD_SIZE] / sums[HEAD_SIZE : HEAD_SIZE + 1]
        ).astype(jnp.bfloat16)

    return sink


def window_mask(extents_ref, places, valid):
    def mask(head, part, scores):
        extent = extents_ref[head, :1, :]
        shape = (LANES, scores.shape[1])
        gap = lax.broadcasted_iota(jnp.int32, shape, 1) - lax.broadcasted_iota(jnp.int32, shape, 0)
        out = []
        for n, (ahead, outer) in enumerate(places[part]):
            reach = jnp.where(valid, extent, -1) if outer else extent
            if ahead <= -LANES:
                seen = gap <= reach + ahead
            elif ahead >= LANES:
                seen = gap >= ahead - reach
            else:
                seen = jnp.abs(gap - ahead) <= reach
            out.append(jnp.where(seen, scores[n * LANES : (n + 1) * LANES], LOW))
        return jnp.concatenate(out, axis=0)

    return mask


def window_parts(rows, begin, end):
    parts, places = [], []
    for row in range(0, rows, LANES):
        near = [k for k in range(begin, end, LANES) if -WIN - LANES < k - row < WIN + LANES]
        near = near or [begin]
        parts.append((row, LANES, near[0] - begin, len(near) * LANES))
        places.append([(k - row, not 0 <= k < rows) for k in near])
    return parts, places


def on_side(parity, run):
    me, last = lax.axis_index("seq"), lax.axis_size("seq") - 1
    is_right = lax.rem(me, 2) == parity
    pl.when(is_right)(lambda: run(True, me < last))
    pl.when(jnp.logical_not(is_right))(lambda: run(False, me > 0))


def own_window_kernel(
    extent_ref, queries_ref, own_ref, even_ref, extents_ref, q_ref, sums_ref, tops_ref, values_ref
):
    rows = own_ref.shape[0]
    for head in range(extents_ref.shape[0]):
        one = splat(extent_ref[...], head, extents_ref.shape[1:])
        extents_ref[head] = one.astype(jnp.int32)
    spread_queries(queries_ref[...], values_ref.shape[0], q_ref)

    def run(right, valid):
        begin, refs = (0, [own_ref, even_ref]) if right else (-WIN, [even_ref, own_ref])
        at = 0
        for ref in refs:
            spread_values(ref[...], values_ref, at)
            at += ref.shape[0]
        parts, places = window_parts(rows, begin, begin + at)
        attend(
            q_ref,
            refs,
            values_ref,
            parts,
            window_mask(extents_ref, places, valid),
            None,
            keep_state(sums_ref, tops_ref),
        )

    on_side(0, run)


def halo_window_kernel(
    extents_ref,
    q_ref,
    odd_ref,
    sums_ref,
    tops_ref,
    residual_ref,
    out_w_ref,
    kv_w_ref,
    hidden_ref,
    normed_ref,
    kv_ref,
    values_ref,
    attended_ref,
):
    rows = q_ref.shape[1]
    spread_values(odd_ref[...], values_ref, 0)

    def run(right, valid):
        begin = rows if right else -WIN
        parts, places = window_parts(rows, begin, begin + WIN)
        attend(
            q_ref,
            [odd_ref],
            values_ref,
            parts,
            window_mask(extents_ref, places, valid),
            (sums_ref, tops_ref),
            keep_heads(attended_ref),
        )

    on_side(1, run)
    def project(here):
        hidden_ref[here, :] = (
            dot_first(attended_ref[:, here], out_w_ref[...])
            + residual_ref[here, :].astype(jnp.float32)
        ).astype(jnp.bfloat16)

    def norm(here):
        values = hidden_ref[here, :].astype(jnp.float32)
        scale = lax.rsqrt(jnp.mean(values * values, axis=-1, keepdims=True) + 1e-05)
        normed = (values * scale).astype(jnp.bfloat16)
        normed_ref[here, :] = normed
        kv_ref[here, :] = dot(normed, kv_w_ref[...]).astype(jnp.bfloat16)

    pieces = [pl.ds(row, PIECE) for row in range(0, rows, PIECE)]
    for n, here in enumerate(pieces):
        project(here)
        if n:
            norm(pieces[n - 1])
    norm(pieces[-1])


def all_seen(head, part, scores):
    return scores


def place_blocks(levels, blocks, own_ref, shown_ref, keys_ref, values_ref, first):
    rows = own_ref.shape[0]
    for n, (level, block) in enumerate(zip(levels, blocks)):
        shown = shown_ref[level, :1, :]
        wide = jnp.concatenate([shown] * (rows // LANES), axis=1)
        for c in range(0, own_ref.shape[1] // 2, LANES):
            keys = block[:, c : c + LANES]
            here = jnp.broadcast_to(shown, keys.shape) > 0
            keys_ref[pl.ds(n * rows, rows), c : c + LANES] = jnp.where(
                here, keys, own_ref[:, c : c + LANES]
            )
        spread_values(block[...], values_ref, first + n * rows, wide)


def own_butterfly_kernel(levels, *refs):
    blocks, refs = refs[: len(levels)], refs[len(levels) :]
    (mask_ref, normed_ref, q_w_ref, own_ref), refs = refs[:4], refs[4:]
    q_ref, sums_ref, tops_ref, shown_ref, values_ref, keys_ref = refs
    rows = normed_ref.shape[0]
    kv_heads = values_ref.shape[0]
    for level in range(shown_ref.shape[0]):
        one = splat(mask_ref[...], level, shown_ref.shape[1:])
        shown_ref[level] = jnp.where(one == 1.0, 1.0, 0.0).astype(jnp.bfloat16)
    spread_queries(
        dot(normed_ref[...], q_w_ref[...]).astype(jnp.bfloat16), kv_heads, q_ref
    )
    spread_values(own_ref[...], values_ref, 0)
    place_blocks(levels, blocks, own_ref, shown_ref, keys_ref, values_ref, rows)
    step = min(rows, ROWS)
    attend(
        q_ref,
        [own_ref, keys_ref],
        values_ref,
        [(row, step, 0, rows * (1 + len(levels))) for row in range(0, rows, step)],
        all_seen,
        None,
        keep_state(sums_ref, tops_ref),
    )


def more_butterfly_kernel(levels, last, *refs):
    blocks, refs = refs[: len(levels)], refs[len(levels) :]
    (shown_ref, own_ref, q_ref, sums_ref, tops_ref), refs = refs[:5], refs[5:]
    rows = q_ref.shape[1]
    if last:
        hidden_ref, out_w_ref, out_ref, values_ref, keys_ref, attended_ref = refs
        sink = keep_heads(attended_ref)
    else:
        sums_out_ref, tops_out_ref, values_ref, keys_ref = refs
        sink = keep_state(sums_out_ref, tops_out_ref)
    place_blocks(levels, blocks, own_ref, shown_ref, keys_ref, values_ref, 0)
    step = min(rows, ROWS)
    attend(
        q_ref,
        [keys_ref],
        values_ref,
        [(row, step, 0, rows * len(levels)) for row in range(0, rows, step)],
        all_seen,
        (sums_ref, tops_ref),
        sink,
    )
    if last:
        out_ref[...] = (
            dot_first(attended_ref[...], out_w_ref[...]) + hidden_ref[...].astype(jnp.float32)
        ).astype(jnp.bfloat16)


def exchange_edges(block, parity):
    groups, count = lax.axis_size("groups"), lax.axis_size("seq")
    rows = block.shape[0]
    if rows > WIN:
        first = jnp.where(lax.rem(lax.axis_index("seq"), 2) == parity, rows - WIN, 0)
        block = lax.dynamic_slice_in_dim(block, first, WIN, 0)
    route = []
    for group in range(groups):
        for i in range(count):
            other, to = group, i + 1 if i % 2 == parity else i - 1
            if not 0 <= to < count:
                other, to = (group ^ 1 if group ^ 1 < groups else group), i
            route.append((group * count + i, other * count + to))
    return lax.ppermute(block, ("groups", "seq"), route)


def shards(
    residual,
    layer_queries,
    layer_keyvals,
    head_window_extent,
    block_mask,
    first_out,
    second_query,
    second_keyval,
    second_out,
):
    rows, width = residual.shape
    q_width = layer_queries.shape[1]
    kv_width = layer_keyvals.shape[1]
    kv_heads = kv_width // (2 * HEAD_SIZE)
    heads = q_width // HEAD_SIZE
    count = lax.axis_size("seq")
    level_count = count.bit_length() - 1
    bf16, f32 = jnp.bfloat16, jnp.float32
    vmem = pl.BlockSpec(memory_space=pltpu.VMEM)
    state = [
        jax.ShapeDtypeStruct((heads, HEAD_SIZE + TOTALS, rows), f32),
        jax.ShapeDtypeStruct((heads, 8, rows), f32),
    ]
    queries = jax.ShapeDtypeStruct((heads, rows, LANES), bf16)
    wide = jax.ShapeDtypeStruct((rows, width), bf16)
    attended = pltpu.VMEM((q_width, rows), bf16)

    def call(kernel, name, in_specs, out_shape, scratch, key_rows, extra_macs, args):
        macs = 4 * rows * heads * HEAD_SIZE * key_rows + extra_macs
        values = pltpu.VMEM((kv_heads, HEAD_SIZE + TOTALS, key_rows), bf16)
        return pl.pallas_call(
            kernel,
            out_shape=out_shape,
            in_specs=in_specs,
            out_specs=jax.tree.map(lambda _: vmem, out_shape),
            scratch_shapes=[values] + scratch,
            compiler_params=pltpu.CompilerParams(vmem_limit_bytes=VMEM_LIMIT),
            cost_estimate=pl.CostEstimate(
                flops=16 * macs, bytes_accessed=2**21, transcendentals=rows * heads * key_rows
            ),
            name=name,
        )(*args)

    even, odd = (exchange_edges(layer_keyvals, parity) for parity in range(2))
    extents, q_here, sums, tops = call(
        own_window_kernel,
        "own_window",
        [vmem] * 4,
        [jax.ShapeDtypeStruct((heads, 8, LANES), jnp.int32), queries] + state,
        [],
        rows + WIN,
        0,
        (head_window_extent.reshape(1, heads), layer_queries, layer_keyvals, even),
    )
    hidden, normed, keyvals = call(
        halo_window_kernel,
        "halo_window",
        [vmem] * 8,
        [wide, wide, jax.ShapeDtypeStruct((rows, kv_width), bf16)],
        [attended],
        WIN,
        rows * width * (q_width + kv_width),
        (
            extents,
            q_here,
            odd,
            sums,
            tops,
            residual,
            first_out,
            second_keyval,
        ),
    )

    others = [None] * level_count
    for level in reversed(range(level_count)):
        route = [(i, i ^ (1 << level)) for i in range(count)]
        others[level] = lax.ppermute(keyvals, "seq", route)
    groups = [[0], [], list(reversed(range(1, level_count)))]
    first, groups = groups[0], [levels for levels in groups[1:] if levels]

    def key_block(levels):
        return pltpu.VMEM((rows * max(len(levels), 1), kv_width // 2), bf16)

    queries_two, sums, tops, shown = call(
        functools.partial(own_butterfly_kernel, first),
        "own_butterfly",
        [vmem] * (4 + len(first)),
        [queries] + state + [jax.ShapeDtypeStruct((level_count, 16, LANES), bf16)],
        [key_block(first)],
        rows * (1 + len(first)),
        rows * width * q_width,
        (*[others[level] for level in first], block_mask, normed, second_query, keyvals),
    )
    for levels in groups[:-1]:
        sums, tops = call(
            functools.partial(more_butterfly_kernel, levels, False),
            "near_butterfly",
            [vmem] * (5 + len(levels)),
            state,
            [key_block(levels)],
            rows * len(levels),
            0,
            (*[others[level] for level in levels], shown, keyvals, queries_two, sums, tops),
        )
    levels = groups[-1]
    return call(
        functools.partial(more_butterfly_kernel, levels, True),
        "far_butterfly",
        [vmem] * (7 + len(levels)),
        wide,
        [key_block(levels), attended],
        rows * len(levels),
        rows * width * q_width,
        (*[others[level] for level in levels], shown, keyvals, queries_two, sums, tops, hidden, second_out),
    )


def solution(mesh):
    tokens = P(("groups", "seq"), None)
    placed = (tokens, tokens, tokens, P(), P("seq", None), P(), P(), P(), P())
    return jax.shard_map(shards, mesh=mesh, in_specs=placed, out_specs=tokens, check_vma=False)
```
